32 devices in a mesh: area: 4 (over z), dev: 8 (over y, x, core).
Axes of the slice: x: 2, y: 2, z: 4, core: 2. Of those that a mesh axis runs over, the one named last changes fastest.
Arguments:
- wave_fwd: float32 [3, 16384, 128], P(None, ('area', 'dev')), may hold values from -6 to 6
- wave_bwd: float32 [3, 16384, 128], P(None, ('area', 'dev')), may hold values from -6 to 6
- seg_reflect: float32 [3, 16384], P(None, ('area', 'dev')), may hold values from 0.04 to 0.4
- seg_count: int32 [32, 64], P(('area', 'dev')), may hold values from 1 to 24, 512 in all within a row
- modal_admit: float32 [3, 2048], P(None, ('area', 'dev')), may hold values from 0.02 to 0.2
- modal_transform: float32 [3, 3], replicated, may hold values from -3.5 to 3.5
- end_slot: int32 [2048, 2], P(('area', 'dev')), may hold values from 0 to 255, as said below
- recv_bus: int32 [32, 256], P(('area', 'dev')), may hold values from -1 to 63, as said below
- bus_impedance: float32 [3, 3, 2048], P(None, None, ('area', 'dev')), as said below
- link_bus: int32 [192, 2], P('area'), may hold values from 0 to 511, as said below
- link_resist: float32 [192], P('area'), may hold values from 0.5 to 5
- source_current: float32 [4, 2048, 3, 128], P(None, ('area', 'dev')), may hold values from -6 to 6
Outputs:
- bus_voltage: float32 [4, 2048, 3, 128], P(None, ('area', 'dev'))
- final_fwd: float32 [3, 16384, 128], P(None, ('area', 'dev'))
- final_bwd: float32 [3, 16384, 128], P(None, ('area', 'dev'))
The draws below stay inside these ranges and needn't reach their ends.
Inputs may be any that keep to these rules, and one draw needn't show every extreme that they name: `end_slot`: entry [l, s] is the slot of end s (0 sending, 1 receiving) of line l within its device's 32 blocks of 8 slots, block q // 8 going to owner device q // 8. The slots of one device are distinct. Every device fills all 8 slots of the block for some owner, and one owner receives 8 ends from every device. `recv_bus`: row r, column s * 8 + c: the local bus of device r to which slot c of device s's block for r attaches, and -1 exactly where no end of device s holds that slot. `link_bus`: the two buses of a link differ. `bus_impedance`: each bus's 3x3 matrix is symmetric with a positive diagonal larger than the sum of its row's other magnitudes.
All inputs are finite; a program needn't handle non-finite values.
Results may differ from the reference program's by a relative error of at most 0.00012.
Values sent between devices are 32-bit elements; how exact they have to be, the bound alone decides.
A program may use at most 64 MiB of HBM per device.

```python
import math
import jax
import jax.numpy as jnp
import numpy as np
from jax import lax

CASES = 128
STEPS = 4
SMAX = 24
LINES_DEV = 64
BUS_DEV = 64
LINK_AREA = 48
SEG_DEV = 512
CAP = 8
BUS_AREA = 512
LINES = 2048
SEGMENTS = 16384
BUSES = 2048
LINKS = 192
N_AREA = 4
DEVICES = 32


def routing_tables(key):
    base = jax.random.fold_in(key, 911)
    key_recv, key_own, key_slots, key_ends, key_bus = jax.random.split(base, 5)
    place_overall_sum = DEVICES * CAP
    every_holder_lookup = jax.random.randint(key_recv, (), 0, DEVICES)
    other = jax.random.randint(key_own, (DEVICES,), 0, DEVICES - 1)
    resident_holder_indicator = jnp.where(other >= every_holder_lookup, other + 1, other)
    place_holder_region = jnp.arange(place_overall_sum, dtype=jnp.int32) // CAP
    ordered_index_list = jax.vmap(lambda sub: jax.random.permutation(sub, place_overall_sum))(jax.random.split(key_slots, DEVICES))
    holder_preference_weight = 2 * (place_holder_region[None, :] == every_holder_lookup).astype(jnp.int32) + (place_holder_region[None, :] == resident_holder_indicator[:, None]).astype(jnp.int32)
    ordered_candidate_items = ordered_index_list.astype(jnp.int32) + place_overall_sum * holder_preference_weight
    top_values, chosen = lax.top_k(ordered_candidate_items, 2 * LINES_DEV)
    shuffle = jax.vmap(lambda sub: jax.random.permutation(sub, 2 * LINES_DEV))(jax.random.split(key_ends, DEVICES))
    picked = jnp.take_along_axis(chosen, shuffle, axis=1)
    rows = jnp.arange(DEVICES, dtype=jnp.int32)[:, None]
    used = jnp.zeros((DEVICES, place_overall_sum), jnp.int32).at[rows, chosen].set(1)
    used = used.reshape(DEVICES, DEVICES, CAP).transpose(1, 0, 2).reshape(DEVICES, place_overall_sum)
    buses = jax.random.randint(key_bus, (DEVICES, place_overall_sum), 0, BUS_DEV)
    received = jnp.where(used == 1, buses, -1)
    return (picked.reshape(DEVICES * LINES_DEV, 2).astype(jnp.int32), received.astype(jnp.int32))


def draw_end_slot(key, part):
    return routing_tables(key)[0]


def draw_recv_bus(key, part):
    return routing_tables(key)[1]


def draw_bus_impedance(key, part):
    key_diag, key_off = jax.random.split(jax.random.fold_in(key, 37), 2)
    diagonal = jax.random.uniform(key_diag, (3, BUSES), jnp.float32, 1.0, 2.0)
    raw = jax.random.uniform(key_off, (3, 3, BUSES), jnp.float32, -0.3, 0.3)
    symmetric = 0.5 * (raw + jnp.transpose(raw, (1, 0, 2)))
    identity = jnp.eye(3, dtype=jnp.float32)[:, :, None]
    matrix = identity * diagonal[None, :, :] + (1.0 - identity) * symmetric
    return matrix.astype(jnp.float32)


def draw_link_bus(key, part):
    key_from, key_gap = jax.random.split(jax.random.fold_in(key, 53), 2)
    start = jax.random.randint(key_from, (LINKS,), 0, BUS_AREA)
    gap = jax.random.randint(key_gap, (LINKS,), 1, BUS_AREA)
    finish = (start + gap) % BUS_AREA
    return jnp.stack([start, finish], axis=1).astype(jnp.int32)


def levels(rng, extent, cuts, least, top_value):
    gain = 1.0
    for dim, parts in cuts:
        draws = jax.random.uniform(jax.random.fold_in(jax.random.fold_in(rng, 6), dim), (parts,), jnp.float32, least / len(cuts), top_value / len(cuts))
        gain = gain * jnp.repeat(jnp.exp(draws), extent[dim] // parts).reshape((-1,) + (1,) * (len(extent) - 1 - dim))
    return gain


def split_up(number_of, total, bound, slope):
    weights = [(1 << 20) // math.isqrt(grade ** slope) + 1 for grade in range(2, number_of + 1)]
    surplus, given = total - bound - (number_of - 1), [1] * (number_of - 1)
    while surplus > 0:
        movable = [i for i in range(number_of - 1) if given[i] < bound]
        pool, budget = sum([weights[i] for i in movable]), surplus
        for i in movable:
            extra = min(bound - given[i], max(1, budget * weights[i] // pool), surplus)
            given[i] = given[i] + extra
            surplus = surplus - extra
    return np.array([bound] + given)


def ragged(rng, count, total, reach, lean):
    if count == 2:
        one = jax.random.randint(rng, (), max(1, total - reach), min(reach, total - 1) + 1)
        return jnp.stack([one, total - one])
    sizes = jnp.asarray(split_up(count, total, reach, lean), jnp.int32)
    pairs = (count - 1) // 2
    donor, receiver = sizes[1:1 + 2 * pairs:2], sizes[2:2 + 2 * pairs:2]
    slack = jnp.minimum(donor - 1, reach - receiver)
    moved = jax.random.randint(jax.random.fold_in(rng, 1), (pairs,), 0, 1 << 20) % (slack + 1)
    sizes = sizes.at[1:1 + 2 * pairs:2].set(donor - moved).at[2:2 + 2 * pairs:2].set(receiver + moved)
    return sizes[jax.random.permutation(jax.random.fold_in(rng, 2), count)]


def normal_values(key, shape, spread, bound, cuts=(), kind=jnp.bfloat16):
    drawn = jax.random.normal(key, shape, jnp.float32) * spread
    if len(cuts) > 0:
        drawn = levels(key, shape, cuts, -0.22, 0.18) * drawn
    return jnp.clip(drawn, min=-bound, max=bound).astype(kind)


def setup_inputs(seed: int = 0) -> dict:
    streams_of = jax.random.split(jax.random.key(seed), 13)
    wave_fwd = normal_values(streams_of[0], (3, SEGMENTS, CASES), 1.0, 6.0, ((1, 32),), jnp.float32)
    wave_bwd = normal_values(streams_of[1], (3, SEGMENTS, CASES), 1.0, 6.0, ((1, 32),), jnp.float32)
    seg_reflect = jnp.clip(jnp.exp(math.log(0.4) - 2.3025851 * jax.random.uniform(streams_of[2], (3, SEGMENTS), jnp.float32) ** levels(streams_of[2], (3, SEGMENTS), ((1, 32),), -0.2, 0.2)), 0.04, 0.4)
    seg_count = jax.vmap(lambda own: ragged(own, LINES_DEV, SEG_DEV, SMAX, 2))(jax.random.split(streams_of[3], DEVICES)).reshape((DEVICES, LINES_DEV)).astype(jnp.int32)
    modal_admit = jnp.clip(jnp.exp(math.log(0.2) - 2.3025851 * jax.random.uniform(streams_of[4], (3, LINES), jnp.float32) ** levels(streams_of[4], (3, LINES), ((1, 32),), -0.2, 0.2)), 0.02, 0.2)
    modal_transform = normal_values(streams_of[5], (3, 3), 3 ** -0.5, 3.5, (), jnp.float32)
    end_slot = draw_end_slot(jax.random.fold_in(streams_of[12], 71), 0)
    recv_bus = draw_recv_bus(jax.random.fold_in(streams_of[12], 71), 0)
    bus_impedance = draw_bus_impedance(jax.random.fold_in(streams_of[12], 71), 0)
    link_bus = draw_link_bus(jax.random.fold_in(streams_of[12], 71), 0)
    link_resist = jnp.clip(jnp.exp(math.log(5.0) - 2.3025851 * jax.random.uniform(streams_of[10], (LINKS,), jnp.float32) ** levels(streams_of[10], (LINKS,), ((0, 4),), -0.2, 0.2)), 0.5, 5.0)
    source_current = normal_values(streams_of[11], (STEPS, BUSES, 3, CASES), 1.0, 6.0, ((1, 32),), jnp.float32)
    return dict(wave_fwd=wave_fwd, wave_bwd=wave_bwd, seg_reflect=seg_reflect, seg_count=seg_count, modal_admit=modal_admit, modal_transform=modal_transform, end_slot=end_slot, recv_bus=recv_bus, bus_impedance=bus_impedance, link_bus=link_bus, link_resist=link_resist, source_current=source_current)


def solve_links(factor, rhs):
    lower = lax.linalg.triangular_solve(factor, rhs, left_side=True, lower=True)
    return lax.linalg.triangular_solve(factor, lower, left_side=True, lower=True, transpose_a=True)

def reference(wave_fwd, wave_bwd, seg_reflect, seg_count, modal_admit, modal_transform, end_slot, recv_bus, bus_impedance, link_bus, link_resist, source_current):
    exact = lax.Precision.HIGHEST
    counts = seg_count.astype(jnp.int32)
    local_first = (jnp.cumsum(counts, axis=1) - counts).astype(jnp.int32)
    offsets = (jnp.arange(DEVICES, dtype=jnp.int32) * SEG_DEV)[:, None]
    first = (local_first + offsets).reshape(-1).astype(jnp.int32)
    last = (first + counts.reshape(-1) - 1).astype(jnp.int32)
    line_device = (jnp.arange(LINES, dtype=jnp.int32) // LINES_DEV)[:, None]
    owner = (end_slot // CAP).astype(jnp.int32)
    column = (line_device * CAP + end_slot % CAP).astype(jnp.int32)
    end_bus = (owner * BUS_DEV + recv_bus[owner, column]).reshape(-1).astype(jnp.int32)
    bus_index = jnp.arange(BUS_AREA, dtype=jnp.int32)
    incidences = []
    factors = []
    for area in range(N_AREA):
        links = link_bus[area * LINK_AREA:(area + 1) * LINK_AREA]
        incidence = (bus_index[:, None] == links[None, :, 0]).astype(jnp.float32) - (bus_index[:, None] == links[None, :, 1]).astype(jnp.float32)
        imped = bus_impedance[:, :, area * BUS_AREA:(area + 1) * BUS_AREA]
        matrix = jnp.einsum('bl,ijb,bm->limj', incidence, imped, incidence, precision=exact).reshape(3 * LINK_AREA, 3 * LINK_AREA)
        matrix = matrix + jnp.diag(jnp.repeat(link_resist[area * LINK_AREA:(area + 1) * LINK_AREA], 3))
        incidences.append(incidence)
        factors.append(jnp.linalg.cholesky(matrix))
    forward, backward = (wave_fwd, wave_bwd)
    reflect = seg_reflect
    reflect_next = jnp.roll(seg_reflect, -1, axis=1)
    voltages = []
    for step in range(STEPS):
        arriving = jnp.stack([backward[:, first, :], forward[:, last, :]], axis=2)
        history = 2.0 * jnp.einsum('mi,mlsk->lsik', modal_transform, modal_admit[:, :, None, None] * arriving, precision=exact)
        summed = jax.ops.segment_sum(history.reshape(2 * LINES, 3, CASES), end_bus, num_segments=BUSES)
        inject = source_current[step] + summed
        open_volts = jnp.einsum('ijb,bjk->bik', bus_impedance, inject, precision=exact)
        pieces = []
        for area in range(N_AREA):
            rows = slice(area * BUS_AREA, (area + 1) * BUS_AREA)
            sources = jnp.einsum('bl,bik->lik', incidences[area], open_volts[rows], precision=exact).reshape(3 * LINK_AREA, CASES)
            current = solve_links(factors[area], sources).reshape(LINK_AREA, 3, CASES)
            pieces.append(inject[rows] - jnp.einsum('bl,lik->bik', incidences[area], current, precision=exact))
        volts = jnp.einsum('ijb,bjk->bik', bus_impedance, jnp.concatenate(pieces, axis=0), precision=exact)
        voltages.append(volts)
        end_volts = volts[end_bus].reshape(LINES, 2, 3, CASES)
        outgoing = jnp.einsum('mi,lsik->mlsk', modal_transform, end_volts, precision=exact) - arriving
        fwd_next = (1.0 - reflect)[:, :, None] * jnp.roll(forward, 1, axis=1) + reflect[:, :, None] * backward
        fwd_next = fwd_next.at[:, first, :].set(outgoing[:, :, 0, :])
        bwd_next = (1.0 - reflect_next)[:, :, None] * jnp.roll(backward, -1, axis=1) + reflect_next[:, :, None] * forward
        bwd_next = bwd_next.at[:, last, :].set(outgoing[:, :, 1, :])
        forward, backward = (fwd_next, bwd_next)
    return (jnp.stack(voltages), forward, backward)
```

```python
import functools

import jax
import jax.numpy as jnp
from jax import lax
from jax.experimental import pallas as pl
from jax.experimental.pallas import tpu as pltpu
from jax.sharding import PartitionSpec as P

STEPS = 4
HALVES = 2
MESH = pl.DeviceIdType.MESH
F32 = jnp.float32
BF16 = jnp.bfloat16
EXACT = lax.Precision.HIGHEST


def iota(shape, dim):
    return lax.broadcasted_iota(jnp.int32, shape, dim)


def to_column(row):
    n = row.shape[1]
    eye = iota((n, n), 0) == iota((n, n), 1)
    return jnp.sum(jnp.where(eye, row, 0.0), axis=1, keepdims=True)


def to_row(column):
    n = column.shape[0]
    eye = iota((n, n), 0) == iota((n, n), 1)
    return jnp.sum(jnp.where(eye, column, 0.0), axis=0, keepdims=True)


def onehot(flag):
    return jnp.where(flag, 1.0, 0.0).astype(BF16)


def high_low(value):
    high = value.astype(BF16)
    return high, (value - high.astype(F32)).astype(BF16)


def pick(matrix, value):
    n = value.shape[1]
    both = jnp.dot(
        matrix, jnp.concatenate(high_low(value), axis=1), preferred_element_type=F32
    )
    return both[:, :n] + both[:, n:]


def swap(value):
    return pltpu.roll(value, value.shape[1] // 2, 1)


def lower(value):
    return iota(value.shape, 1) < value.shape[1] // 2


def pack(value):
    n = value.shape[0] // 2
    top, bottom = value[:n], value[n:]
    left = lower(top)
    return jnp.where(left, top, swap(bottom)), jnp.where(left, swap(top), bottom)


def unpack(first, second):
    left = lower(first)
    return jnp.concatenate(
        [jnp.where(left, first, swap(second)), jnp.where(left, swap(first), second)], axis=0
    )


def fold(result):
    m = result.shape[0] // 4
    tl, tr, bl, br = (result[k * m : (k + 1) * m] for k in range(4))
    left = lower(tl)
    return jnp.where(left, tl, br) + swap(jnp.where(left, bl, tr))


def packed_dot(table, parts):
    n = parts[0].shape[1]
    both = jnp.concatenate(high_low(jnp.concatenate(parts, axis=1)), axis=0)
    result = jnp.dot(table, both, preferred_element_type=F32)
    return [fold(result[:, k * n : (k + 1) * n]) for k in range(len(parts))]


def kernel(
    areas,
    devs,
    fwd_in,
    bwd_in,
    refl_ref,
    count_ref,
    admit_ref,
    trans_ref,
    slot_ref,
    recv_ref,
    imp_ref,
    link_ref,
    resist_ref,
    src_in,
    volt_out,
    fwd_out,
    bwd_out,
    fwd,
    bwd,
    src,
    volt,
    h_send,
    h_recv,
    e_recv,
    v_send,
    v_recv,
    imp_all,
    zrow,
    ends_of,
    swap_of,
    gbt,
    gft,
    rsum,
    rback,
    ct,
    u,
    adm,
    zpack,
    spack,
    keep_f,
    take_f,
    keep_b,
    take_b,
    arr,
    nxt,
    out,
    open_volts,
    minv,
    send_sem,
    recv_sem,
    imp_sem,
    in_sem,
    out_sem,
):
    total = areas * devs
    area, dev = lax.axis_index("area"), lax.axis_index("dev")
    me = area * devs + dev
    cases = fwd.shape[2]
    segs = fwd.shape[1]
    lines = slot_ref.shape[1]
    slots = recv_ref.shape[1]
    buses = imp_ref.shape[2]
    links = link_ref.shape[1]
    rows = slots // total
    few = rows // 2
    packed = slots // 2
    near = buses // 2
    some = links // 2

    inputs = [
        pltpu.make_async_copy(a, b, in_sem.at[k])
        for k, (a, b) in enumerate(((fwd_in, fwd), (bwd_in, bwd), (src_in, src)))
    ]
    for copy in inputs:
        copy.start()

    barrier = pltpu.get_barrier_semaphore()

    def peer_of(p):
        peer = lax.rem(me + p, total)
        return peer, (peer // devs, lax.rem(peer, devs))

    @pl.loop(1, total)
    def _(p):
        _, where = peer_of(p)
        pl.semaphore_signal(barrier, inc=1, device_id=where, device_id_type=MESH)

    def push_all(send, recv, phase, step, h):
        @pl.loop(1, total, unroll=total <= 32)
        def _(p):
            peer, where = peer_of(p)
            pltpu.make_async_remote_copy(
                src_ref=send.at[step, h, peer],
                dst_ref=recv.at[step, h, me],
                send_sem=send_sem.at[phase, step, h],
                recv_sem=recv_sem.at[phase, step, h],
                device_id=where,
                device_id_type=MESH,
            ).start()

        recv[step, h, me] = send[step, h, me]

    def wait(buf, count, sem):
        ref = buf.at[pl.ds(0, count)]
        pltpu.make_async_copy(ref, ref, sem).wait()

    def place(slot):
        bits = few.bit_length() - 1
        upper = lax.shift_right_logical(slot, bits)
        return (upper & 1) * packed + lax.shift_right_logical(upper, 1) * few + (slot & (few - 1))

    counts_row = count_ref[...].astype(F32)
    counts_col = to_column(counts_row)
    square = (lines, lines)
    first_col = jnp.sum(
        jnp.where(iota(square, 1) < iota(square, 0), counts_row, 0.0), axis=1, keepdims=True
    )
    last_col = first_col + counts_col - 1.0
    slot0_row = place(slot_ref[0:1, :]).astype(F32)
    slot1_row = place(slot_ref[1:2, :]).astype(F32)
    seg_lane = iota((lines, segs), 1).astype(F32)
    slot_sub = iota((slots, lines), 0).astype(F32)
    q0, q1 = onehot(slot_sub == slot0_row), onehot(slot_sub == slot1_row)
    ends_of[:, :segs] = jnp.dot(
        q0, onehot(seg_lane == first_col), preferred_element_type=F32
    ).astype(BF16)
    ends_of[:, segs:] = jnp.dot(
        q1, onehot(seg_lane == last_col), preferred_element_type=F32
    ).astype(BF16)
    held = q0.astype(F32) + q1.astype(F32)
    for m in range(3):
        column = 2.0 * jnp.sum(held * admit_ref[m : m + 1, :], axis=1, keepdims=True)
        wide = jnp.broadcast_to(column, (slots, cases))
        adm[m] = jnp.where(lower(wide[:packed]), wide[:packed], wide[packed:])

    def gather(target):
        for m in range(3):
            both = jnp.concatenate([bwd[m], fwd[m]], axis=0)
            for h, half in enumerate(pack(pick(ends_of[...], both))):
                target[h, m] = half

    def inject(step, h):
        for i in range(3):
            value = trans_ref[0, i] * (adm[0] * arr[h, 0])
            value = value + trans_ref[1, i] * (adm[1] * arr[h, 1])
            value = value + trans_ref[2, i] * (adm[2] * arr[h, 2])
            h_send[step, h, :, i] = value.reshape(total, few, cases)

    inputs[0].wait()
    inputs[1].wait()
    gather(arr)
    for h in range(HALVES):
        inject(0, h)
    pl.semaphore_wait(barrier, total - 1)

    @pl.loop(1, devs)
    def _(p):
        other = lax.rem(dev + p, devs)
        pltpu.make_async_remote_copy(
            src_ref=imp_ref,
            dst_ref=imp_all.at[dev],
            send_sem=imp_sem.at[0],
            recv_sem=imp_sem.at[1],
            device_id=(area, other),
            device_id_type=MESH,
        ).start()

    for h in range(HALVES):
        push_all(h_send, h_recv, 0, 0, h)
    imp_all[dev] = imp_ref[...]

    recv_placed = jnp.where(
        iota((slots, slots), 0) == place(iota((slots, slots), 1)), recv_ref[...].astype(F32), 0.0
    )
    recv_col = jnp.sum(recv_placed, axis=1, keepdims=True)
    recv_row = to_row(recv_col)
    for k in range(4):
        side = slice((k % 2) * packed, (k % 2 + 1) * packed)
        bus = (iota((near, packed), 0) + (k // 2) * near).astype(F32)
        block = onehot(bus == recv_row[:, side])
        for w in range(2):
            rsum[k * near : (k + 1) * near, w * packed : (w + 1) * packed] = block
        side = slice((k // 2) * packed, (k // 2 + 1) * packed)
        bus = ((iota((packed, 2 * near), 1) & (near - 1)) + (k % 2) * near).astype(F32)
        rback[k * packed : (k + 1) * packed, :] = onehot(bus == recv_col[side])

    link0_row, link1_row = link_ref[0:1, :].astype(F32), link_ref[1:2, :].astype(F32)
    link0, link1 = to_column(link0_row), to_column(link1_row)

    def incidence(index, a, b):
        index = index.astype(F32)
        return jnp.where(index == a, 1.0, 0.0) - jnp.where(index == b, 1.0, 0.0)

    blocks = []
    for k in range(4):
        side = slice((k // 2) * some, (k // 2 + 1) * some)
        bus = (iota((some, 2 * near), 1) & (near - 1)) + (k % 2) * near + dev * buses
        blocks.append(incidence(bus, link0[side], link1[side]))
    ct[...] = jnp.concatenate(blocks, axis=0).astype(BF16)
    zcols = [to_column(imp_ref[ij // 3, ij % 3 : ij % 3 + 1, :]) for ij in range(9)]
    for ij in range(9):
        wide = jnp.broadcast_to(zcols[ij], (buses, cases))
        zpack[ij] = jnp.where(lower(wide[:near]), wide[:near], wide[near:])
    inputs[2].wait()

    @pl.loop(0, STEPS)
    def _(step):
        for i in range(3):
            for h, half in enumerate(pack(src[step, i])):
                spack[step, h, i] = half

    def wave_tables():
        first_row, last_row = to_row(first_col), to_row(last_col)
        slot0_col, slot1_col = to_column(slot0_row), to_column(slot1_row)
        seg_sub = iota((segs, lines), 0).astype(F32)
        slot_lane = iota((lines, slots), 1).astype(F32)
        fst = onehot(seg_sub == first_row)
        lst = onehot(seg_sub == last_row)
        gbt[...] = jnp.dot(
            fst, onehot(slot_lane == slot0_col), preferred_element_type=F32
        ).astype(BF16)
        gft[...] = jnp.dot(
            lst, onehot(slot_lane == slot1_col), preferred_element_type=F32
        ).astype(BF16)
        not_first = 1.0 - jnp.sum(fst.astype(F32), axis=1, keepdims=True)
        not_last = 1.0 - jnp.sum(lst.astype(F32), axis=1, keepdims=True)
        for m in range(3):
            r = to_column(refl_ref[m : m + 1, :])
            r_next = pltpu.roll(jnp.broadcast_to(r, (segs, cases)), segs - 1, 0)
            keep_f[m] = jnp.broadcast_to((1.0 - r) * not_first, (segs, cases))
            take_f[m] = jnp.broadcast_to(r * not_first, (segs, cases))
            keep_b[m] = (1.0 - r_next) * not_last
            take_b[m] = r_next * not_last
        single = jnp.where(counts_row == 1.0, 1.0, 0.0)
        a, b = q0.astype(F32) * single, q1.astype(F32) * single
        across = (((1,), (1,)), ((), ()))
        swaps = lax.dot_general(a.astype(BF16), q1, across, preferred_element_type=F32)
        swaps = swaps + lax.dot_general(b.astype(BF16), q0, across, preferred_element_type=F32)
        swaps = swaps.astype(BF16)
        for k in range(4):
            block = swaps[
                (k // 2) * packed : (k // 2 + 1) * packed, (k % 2) * packed : (k % 2 + 1) * packed
            ]
            for w in range(2):
                swap_of[k * packed : (k + 1) * packed, w * packed : (w + 1) * packed] = block

    def advance():
        for m in range(3):
            f, b = fwd[m], bwd[m]
            fwd[m] = keep_f[m] * pltpu.roll(f, 1, 0) + take_f[m] * b
            bwd[m] = keep_b[m] * pltpu.roll(b, segs - 1, 0) + take_b[m] * f

    def scatter(m):
        value = unpack(out[0, m], out[1, m])
        fwd[m] += pick(gbt[...], value)
        bwd[m] += pick(gft[...], value)

    def form_links():
        wait(imp_all, devs - 1, imp_sem.at[1])
        for d in range(devs):
            for i in range(3):
                zrow[3 * i : 3 * i + 3, d * buses : (d + 1) * buses] = imp_all[d, i]
        c = incidence(iota((links, devs * buses), 1), link0, link1)
        c_exact = c.astype(BF16)
        eye = iota((links, links), 0) == iota((links, links), 1)
        for i in range(3):
            for j in range(i + 1):
                z = zrow[3 * i + j : 3 * i + j + 1, :]
                high = z.astype(BF16).astype(F32)
                mid = (z - high).astype(BF16).astype(F32)
                terms = jnp.concatenate([c * high, c * mid, c * (z - high - mid)], axis=0)
                terms = lax.dot_general(
                    terms.astype(BF16), c_exact, (((1,), (1,)), ((), ())), preferred_element_type=F32
                )
                block = terms[:links] + terms[links : 2 * links] + terms[2 * links :]
                here = slice(i * links, (i + 1) * links)
                past = slice(j * links, (j + 1) * links)
                if i == j:
                    block = block + jnp.where(eye, resist_ref[...], 0.0)
                else:
                    minv[past, here] = block
                minv[here, past] = block

    order = 3 * links
    lane = iota((order, order), 1)

    def eliminate(start, stop):
        @pl.loop(start, stop)
        def _(n):
            spots = [n + w * links for w in range(3)]
            a = minv[...]
            lines_ = [minv[pl.ds(k, 1), :] for k in spots]
            here = [lane == k for k in spots]
            edge = [lane[:1] == k for k in spots]
            cols = [jnp.sum(jnp.where(g, a, 0.0), axis=1, keepdims=True) for g in here]
            block = [
                [jnp.sum(jnp.where(g, r, 0.0), axis=1, keepdims=True) for g in edge]
                for r in lines_
            ]
            for v in range(3):
                inverse = 1.0 / block[v][v]
                row, col = lines_[v], cols[v] * inverse
                a = a - col * row
                scaled = row * inverse
                factor = [block[w][v] for w in range(3)]
                across = [block[v][w] * inverse for w in range(3)]
                for w in range(3):
                    lines_[w] = scaled if w == v else lines_[w] - factor[w] * scaled
                    cols[w] = col if w == v else cols[w] - block[v][w] * col
                for w in range(3):
                    for x in range(3):
                        if w != v and x != v:
                            block[w][x] = block[w][x] - factor[w] * across[x]
                for w in range(3):
                    if w != v:
                        block[w][v], block[v][w] = factor[w] * inverse, across[w]
                block[v][v] = -inverse
            for w in range(3):
                a = jnp.where(here[w], cols[w], a)
                for x in range(3):
                    lines_[w] = jnp.where(edge[x], block[w][x], lines_[w])
            minv[...] = a
            for w in range(3):
                minv[pl.ds(spots[w], 1), :] = lines_[w]

    def link_effect():
        source, target = iota((order, 2 * cases), 0), iota((order, 2 * cases), 1)
        side, spot = target // cases, target % cases
        wanted = (spot // some) * links + side * some + spot % some
        chosen = jnp.where((source == wanted) & (spot < 3 * some), 1.0, 0.0)
        inverse = jnp.dot(minv[...], chosen, precision=EXACT, preferred_element_type=F32)
        c = incidence(iota((buses, links), 0) + dev * buses, link0_row, link1_row)
        drops = [
            jnp.dot(
                c,
                inverse[k * links : (k + 1) * links],
                precision=EXACT,
                preferred_element_type=F32,
            )
            for k in range(3)
        ]
        for i in range(3):
            effect = zcols[3 * i] * drops[0] + zcols[3 * i + 1] * drops[1]
            effect = effect + zcols[3 * i + 2] * drops[2]
            for w, part in enumerate(high_low(effect)):
                for k in range(4):
                    spot = (4 * w + k) * 3 * near + i * near
                    u[spot : spot + near, :] = part[
                        (k // 2) * near : (k // 2 + 1) * near,
                        (k % 2) * cases : (k % 2) * cases + 3 * some,
                    ]

    def apply(values):
        return [
            zpack[3 * i] * values[0] + zpack[3 * i + 1] * values[1] + zpack[3 * i + 2] * values[2]
            for i in range(3)
        ]

    def share(step, h):
        wait(h_recv.at[step, h], total - 1, recv_sem.at[0, step, h])
        parts = [h_recv[step, h, :, i].reshape(packed, cases) for i in range(3)]
        total_in = packed_dot(rsum[...], parts)
        volts = apply([spack[step, h, i] + total_in[i] for i in range(3)])
        for i in range(3):
            open_volts[h, i] = volts[i]
        opened = packed_dot(ct[...], volts)
        for i in range(3):
            e_recv[step, h, dev, i * some : (i + 1) * some, :] = opened[i]

        @pl.loop(1, devs, unroll=devs <= 8)
        def _(p):
            pltpu.make_async_remote_copy(
                src_ref=e_recv.at[step, h, dev],
                dst_ref=e_recv.at[step, h, dev],
                send_sem=send_sem.at[1, step, h],
                recv_sem=recv_sem.at[1, step, h],
                device_id=(area, lax.rem(dev + p, devs)),
                device_id_type=MESH,
            ).start()

    def settle(step, h):
        wait(e_recv.at[step, h], devs - 1, recv_sem.at[1, step, h])
        opened = jnp.sum(e_recv[step, h], axis=0)
        result = jnp.dot(
            u[...], jnp.concatenate(high_low(opened), axis=1), preferred_element_type=F32
        )
        main = 12 * near
        change = fold(result[:main, :cases] + result[:main, cases:] + result[main:, :cases])
        volts = [open_volts[h, i] + change[i * near : (i + 1) * near] for i in range(3)]
        half = cases // 2
        mine = slice(h * half, (h + 1) * half)
        for i in range(3):
            turned = swap(volts[i])
            low, high = (volts[i], turned) if h == 0 else (turned, volts[i])
            volt[step, i, :near, mine] = low[:, mine]
            volt[step, i, near:, mine] = high[:, mine]
        sent = packed_dot(rback[...], volts)
        for i in range(3):
            v_send[step, h, :, i] = sent[i].reshape(total, few, cases)
        push_all(v_send, v_recv, 2, step, h)

    def leave(step, h):
        wait(v_recv.at[step, h], total - 1, recv_sem.at[2, step, h])
        ends = [v_recv[step, h, :, i].reshape(packed, cases) for i in range(3)]
        results = []
        for m in range(3):
            value = trans_ref[m, 0] * ends[0] + trans_ref[m, 1] * ends[1] + trans_ref[m, 2] * ends[2]
            value = value - arr[h, m]
            out[h, m] = value
            results.append(value)
        return results

    def volt_copy(step):
        return pltpu.make_async_copy(volt.at[step], volt_out.at[step], out_sem.at[step])

    form_links()
    eliminate(0, links // 4)
    for h in range(HALVES):
        share(0, h)
    eliminate(links // 4, links)
    link_effect()
    for h in range(HALVES):
        settle(0, h)
    volt_copy(0).start()
    wave_tables()
    advance()
    gather(nxt)

    @pl.loop(1, STEPS)
    def _(step):
        for h in range(HALVES):
            moved = packed_dot(swap_of[...], leave(step - 1, h))
            for m in range(3):
                arr[h, m] = nxt[h, m] + moved[m]
            inject(step, h)
            push_all(h_send, h_recv, 0, step, h)
        for m in range(3):
            scatter(m)
        advance()

        @pl.when(step < STEPS - 1)
        def _():
            gather(nxt)

        for h in range(HALVES):
            share(step, h)
        for h in range(HALVES):
            settle(step, h)
        volt_copy(step).start()

    for h in range(HALVES):
        leave(STEPS - 1, h)
    outputs = []
    for m in range(3):
        scatter(m)
        for k, (a, b) in enumerate(((fwd, fwd_out), (bwd, bwd_out))):
            outputs.append(
                pltpu.make_async_copy(a.at[m], b.at[m], out_sem.at[STEPS + 2 * m + k])
            )
            outputs[-1].start()

    wait(imp_all, devs - 1, imp_sem.at[0])

    @pl.loop(0, STEPS)
    def _(step):
        volt_copy(step).wait()
        for h in range(HALVES):
            wait(h_send.at[step, h], total - 1, send_sem.at[0, step, h])
            wait(e_recv.at[step, h], devs - 1, send_sem.at[1, step, h])
            wait(v_send.at[step, h], total - 1, send_sem.at[2, step, h])

    for copy in outputs:
        copy.wait()


def hand_over(volt_in, fwd_in, bwd_in, volt_out, fwd_out, bwd_out, volt, fwd, bwd, sems):
    groups = ((fwd_in, fwd, fwd_out), (bwd_in, bwd, bwd_out), (volt_in, volt, volt_out))
    copies = [
        (
            pltpu.make_async_copy(a.at[n], b.at[n], sems.at[0, k, n]),
            pltpu.make_async_copy(b.at[n], c.at[n], sems.at[1, k, n]),
        )
        for k, (a, b, c) in enumerate(groups)
        for n in range(a.shape[0])
    ]
    for first, _ in copies:
        first.start()
    for first, second in copies:
        first.wait()
        second.start()
    for _, second in copies:
        second.wait()


def on_device(
    areas,
    devs,
    wave_fwd,
    wave_bwd,
    seg_reflect,
    seg_count,
    modal_admit,
    modal_transform,
    end_slot,
    recv_bus,
    bus_impedance,
    link_bus,
    link_resist,
    source_current,
):
    total = areas * devs
    cases, segs = wave_fwd.shape[2], wave_fwd.shape[1]
    cap = recv_bus.shape[1] // total
    rows = -(-cap // 8) * 8
    if rows != cap:
        end_slot = end_slot // cap * rows + end_slot % cap
        recv_bus = jnp.pad(
            recv_bus.reshape(total, cap), ((0, 0), (0, rows - cap)), constant_values=-1
        ).reshape(1, total * rows)
    slots = total * rows
    buses = bus_impedance.shape[2]
    links = link_bus.shape[0]
    vmem = pl.BlockSpec(memory_space=pltpu.VMEM)
    smem = pl.BlockSpec(memory_space=pltpu.SMEM)
    anywhere = pl.BlockSpec(memory_space=pl.ANY)
    volt_shape = (STEPS, 3, buses, cases)
    sent = (STEPS, HALVES, total, 3, rows // 2, cases)
    half_slots = (HALVES, 3, slots // 2, cases)
    results = pl.pallas_call(
        functools.partial(kernel, areas, devs),
        out_shape=(
            jax.ShapeDtypeStruct(volt_shape, F32),
            jax.ShapeDtypeStruct(wave_fwd.shape, F32),
            jax.ShapeDtypeStruct(wave_bwd.shape, F32),
        ),
        in_specs=[anywhere] * 2 + [vmem] * 3 + [smem] + [vmem] * 5 + [anywhere],
        out_specs=(anywhere, anywhere, anywhere),
        scratch_shapes=[
            pltpu.VMEM(wave_fwd.shape, F32),
            pltpu.VMEM(wave_bwd.shape, F32),
            pltpu.VMEM(volt_shape, F32),
            pltpu.VMEM(volt_shape, F32),
            pltpu.VMEM(sent, F32),
            pltpu.VMEM(sent, F32),
            pltpu.VMEM((STEPS, HALVES, devs, 3 * links // 2, cases), F32),
            pltpu.VMEM(sent, F32),
            pltpu.VMEM(sent, F32),
            pltpu.VMEM((devs, 3, 3, buses), F32),
            pltpu.VMEM((16, devs * buses), F32),
            pltpu.VMEM((slots, 2 * segs), BF16),
            pltpu.VMEM((2 * slots, slots), BF16),
            pltpu.VMEM((segs, slots), BF16),
            pltpu.VMEM((segs, slots), BF16),
            pltpu.VMEM((2 * buses, slots), BF16),
            pltpu.VMEM((2 * slots, buses), BF16),
            pltpu.VMEM((2 * links, buses), BF16),
            pltpu.VMEM((12 * buses, 3 * links // 2), BF16),
            pltpu.VMEM((3, slots // 2, cases), F32),
            pltpu.VMEM((9, buses // 2, cases), F32),
            pltpu.VMEM((STEPS, HALVES, 3, buses // 2, cases), F32),
            pltpu.VMEM((3, segs, cases), F32),
            pltpu.VMEM((3, segs, cases), F32),
            pltpu.VMEM((3, segs, cases), F32),
            pltpu.VMEM((3, segs, cases), F32),
            pltpu.VMEM(half_slots, F32),
            pltpu.VMEM(half_slots, F32),
            pltpu.VMEM(half_slots, F32),
            pltpu.VMEM((HALVES, 3, buses // 2, cases), F32),
            pltpu.VMEM((3 * links, 3 * links), F32),
            pltpu.SemaphoreType.DMA((3, STEPS, HALVES)),
            pltpu.SemaphoreType.DMA((3, STEPS, HALVES)),
            pltpu.SemaphoreType.DMA((2,)),
            pltpu.SemaphoreType.DMA((3,)),
            pltpu.SemaphoreType.DMA((STEPS + 6,)),
        ],
        compiler_params=pltpu.CompilerParams(
            collective_id=0, has_side_effects=True, vmem_limit_bytes=60 * 1024 * 1024
        ),
        name="transient",
    )(
        wave_fwd,
        wave_bwd,
        seg_reflect,
        seg_count,
        modal_admit,
        modal_transform,
        end_slot.T,
        recv_bus,
        bus_impedance,
        link_bus.T,
        link_resist.reshape(1, links),
        jnp.transpose(source_current, (0, 2, 1, 3)),
    )
    volts, fwd, bwd = pl.pallas_call(
        hand_over,
        out_shape=tuple(jax.ShapeDtypeStruct(a.shape, F32) for a in results),
        in_specs=[anywhere] * 3,
        out_specs=(anywhere,) * 3,
        scratch_shapes=[pltpu.VMEM(a.shape, F32) for a in results]
        + [pltpu.SemaphoreType.DMA((2, 3, STEPS))],
        name="hand_over",
    )(*results)
    return (jnp.transpose(volts, (0, 2, 1, 3)), fwd, bwd)


def solution(mesh):
    in_specs = (
        P(None, ("area", "dev"), None),
        P(None, ("area", "dev"), None),
        P(None, ("area", "dev")),
        P(("area", "dev"), None),
        P(None, ("area", "dev")),
        P(),
        P(("area", "dev"), None),
        P(("area", "dev"), None),
        P(None, None, ("area", "dev")),
        P("area", None),
        P("area"),
        P(None, ("area", "dev"), None, None),
    )
    out_specs = (
        P(None, ("area", "dev"), None, None),
        P(None, ("area", "dev"), None),
        P(None, ("area", "dev"), None),
    )
    return jax.shard_map(
        functools.partial(on_device, mesh.shape["area"], mesh.shape["dev"]),
        mesh=mesh,
        in_specs=in_specs,
        out_specs=out_specs,
        check_vma=False,
    )
```

```python
import functools

import jax
import jax.numpy as jnp
from jax import lax
from jax.experimental import pallas as pl
from jax.experimental.pallas import tpu as pltpu
from jax.sharding import PartitionSpec as P

STEPS = 4
HALVES = 2
MESH = pl.DeviceIdType.MESH
F32 = jnp.float32
BF16 = jnp.bfloat16
EXACT = lax.Precision.HIGHEST


def iota(shape, dim):
    return lax.broadcasted_iota(jnp.int32, shape, dim)


def to_column(row):
    n = row.shape[1]
    eye = iota((n, n), 0) == iota((n, n), 1)
    return jnp.sum(jnp.where(eye, row, 0.0), axis=1, keepdims=True)


def to_row(column):
    n = column.shape[0]
    eye = iota((n, n), 0) == iota((n, n), 1)
    return jnp.sum(jnp.where(eye, column, 0.0), axis=0, keepdims=True)


def onehot(flag):
    return jnp.where(flag, 1.0, 0.0).astype(BF16)


def high_low(value):
    high = value.astype(BF16)
    return high, (value - high.astype(F32)).astype(BF16)


def pick(matrix, value):
    n = value.shape[1]
    both = jnp.dot(
        matrix, jnp.concatenate(high_low(value), axis=1), preferred_element_type=F32
    )
    return both[:, :n] + both[:, n:]


def swap(value):
    return pltpu.roll(value, value.shape[1] // 2, 1)


def lower(value):
    return iota(value.shape, 1) < value.shape[1] // 2


def pack(value):
    n = value.shape[0] // 2
    top, bottom = value[:n], value[n:]
    left = lower(top)
    return jnp.where(left, top, swap(bottom)), jnp.where(left, swap(top), bottom)


def unpack(first, second):
    left = lower(first)
    return jnp.concatenate(
        [jnp.where(left, first, swap(second)), jnp.where(left, swap(first), second)], axis=0
    )


def fold(result):
    m = result.shape[0] // 4
    tl, tr, bl, br = (result[k * m : (k + 1) * m] for k in range(4))
    left = lower(tl)
    return jnp.where(left, tl, br) + swap(jnp.where(left, bl, tr))


def packed_dot(table, parts):
    n = parts[0].shape[1]
    both = jnp.concatenate(high_low(jnp.concatenate(parts, axis=1)), axis=0)
    result = jnp.dot(table, both, preferred_element_type=F32)
    return [fold(result[:, k * n : (k + 1) * n]) for k in range(len(parts))]


def kernel(
    areas,
    devs,
    fwd_in,
    bwd_in,
    refl_ref,
    count_ref,
    admit_ref,
    trans_ref,
    slot_ref,
    recv_ref,
    imp_ref,
    link_ref,
    resist_ref,
    src_in,
    volt_out,
    fwd_out,
    bwd_out,
    fwd,
    bwd,
    src,
    volt,
    h_send,
    h_recv,
    e_recv,
    v_send,
    v_recv,
    imp_all,
    zrow,
    ends_of,
    swap_of,
    gbt,
    gft,
    rsum,
    rback,
    ct,
    u,
    adm,
    zpack,
    spack,
    keep_f,
    take_f,
    keep_b,
    take_b,
    arr,
    nxt,
    out,
    open_volts,
    near_inv,
    cross,
    cross_back,
    far_inv,
    ahead,
    inverse,
    send_sem,
    recv_sem,
    imp_sem,
    in_sem,
    out_sem,
):
    total = areas * devs
    area, dev = lax.axis_index("area"), lax.axis_index("dev")
    me = area * devs + dev
    cases = fwd.shape[2]
    segs = fwd.shape[1]
    lines = slot_ref.shape[1]
    slots = recv_ref.shape[1]
    buses = imp_ref.shape[2]
    links = link_ref.shape[1]
    rows = slots // total
    few = rows // 2
    packed = slots // 2
    near = buses // 2
    some = links // 2

    inputs = [
        pltpu.make_async_copy(a, b, in_sem.at[k])
        for k, (a, b) in enumerate(((fwd_in, fwd), (bwd_in, bwd), (src_in, src)))
    ]
    for copy in inputs:
        copy.start()

    barrier = pltpu.get_barrier_semaphore()

    def peer_of(p):
        other_area = area ^ (areas - 1 - lax.rem(p, areas))
        other_dev = dev ^ (devs - 1 - p // areas)
        return other_area * devs + other_dev, (other_area, other_dev)

    @pl.loop(0, total - 1)
    def _(p):
        _, where = peer_of(p)
        pl.semaphore_signal(barrier, inc=1, device_id=where, device_id_type=MESH)

    def push_all(send, recv, phase, step, h):
        @pl.loop(0, total - 1, unroll=total <= 32)
        def _(p):
            peer, where = peer_of(p)
            pltpu.make_async_remote_copy(
                src_ref=send.at[step, h, peer],
                dst_ref=recv.at[step, h, me],
                send_sem=send_sem.at[phase, step, h],
                recv_sem=recv_sem.at[phase, step, h],
                device_id=where,
                device_id_type=MESH,
            ).start()

        recv[step, h, me] = send[step, h, me]

    def wait(buf, count, sem):
        ref = buf.at[pl.ds(0, count)]
        pltpu.make_async_copy(ref, ref, sem).wait()

    def place(slot):
        bits = few.bit_length() - 1
        upper = lax.shift_right_logical(slot, bits)
        return (upper & 1) * packed + lax.shift_right_logical(upper, 1) * few + (slot & (few - 1))

    counts_row = count_ref[...].astype(F32)
    counts_col = to_column(counts_row)
    square = (lines, lines)
    first_col = jnp.sum(
        jnp.where(iota(square, 1) < iota(square, 0), counts_row, 0.0), axis=1, keepdims=True
    )
    last_col = first_col + counts_col - 1.0
    slot0_row = place(slot_ref[0:1, :]).astype(F32)
    slot1_row = place(slot_ref[1:2, :]).astype(F32)
    seg_lane = iota((lines, segs), 1).astype(F32)
    slot_sub = iota((slots, lines), 0).astype(F32)
    q0, q1 = onehot(slot_sub == slot0_row), onehot(slot_sub == slot1_row)
    ends_of[:, :segs] = jnp.dot(
        q0, onehot(seg_lane == first_col), preferred_element_type=F32
    ).astype(BF16)
    ends_of[:, segs:] = jnp.dot(
        q1, onehot(seg_lane == last_col), preferred_element_type=F32
    ).astype(BF16)
    held = q0.astype(F32) + q1.astype(F32)
    for m in range(3):
        column = 2.0 * jnp.sum(held * admit_ref[m : m + 1, :], axis=1, keepdims=True)
        wide = jnp.broadcast_to(column, (slots, cases))
        adm[m] = jnp.where(lower(wide[:packed]), wide[:packed], wide[packed:])

    def gather(target):
        for m in range(3):
            both = jnp.concatenate([bwd[m], fwd[m]], axis=0)
            for h, half in enumerate(pack(pick(ends_of[...], both))):
                target[h, m] = half

    def inject(step, h):
        for i in range(3):
            value = trans_ref[0, i] * (adm[0] * arr[h, 0])
            value = value + trans_ref[1, i] * (adm[1] * arr[h, 1])
            value = value + trans_ref[2, i] * (adm[2] * arr[h, 2])
            h_send[step, h, :, i] = value.reshape(total, few, cases)

    inputs[0].wait()
    inputs[1].wait()
    gather(arr)
    for h in range(HALVES):
        inject(0, h)
    pl.semaphore_wait(barrier, total - 1)

    @pl.loop(1, devs)
    def _(p):
        other = lax.rem(dev + p, devs)
        pltpu.make_async_remote_copy(
            src_ref=imp_ref,
            dst_ref=imp_all.at[dev],
            send_sem=imp_sem.at[0],
            recv_sem=imp_sem.at[1],
            device_id=(area, other),
            device_id_type=MESH,
        ).start()

    for h in range(HALVES):
        push_all(h_send, h_recv, 0, 0, h)
    imp_all[dev] = imp_ref[...]

    recv_placed = jnp.where(
        iota((slots, slots), 0) == place(iota((slots, slots), 1)), recv_ref[...].astype(F32), 0.0
    )
    recv_col = jnp.sum(recv_placed, axis=1, keepdims=True)
    recv_row = to_row(recv_col)
    for k in range(4):
        side = slice((k % 2) * packed, (k % 2 + 1) * packed)
        bus = (iota((near, packed), 0) + (k // 2) * near).astype(F32)
        block = onehot(bus == recv_row[:, side])
        for w in range(2):
            rsum[k * near : (k + 1) * near, w * packed : (w + 1) * packed] = block
        side = slice((k // 2) * packed, (k // 2 + 1) * packed)
        bus = ((iota((packed, 2 * near), 1) & (near - 1)) + (k % 2) * near).astype(F32)
        rback[k * packed : (k + 1) * packed, :] = onehot(bus == recv_col[side])

    link0_row, link1_row = link_ref[0:1, :].astype(F32), link_ref[1:2, :].astype(F32)
    link0, link1 = to_column(link0_row), to_column(link1_row)

    def incidence(index, a, b):
        index = index.astype(F32)
        return jnp.where(index == a, 1.0, 0.0) - jnp.where(index == b, 1.0, 0.0)

    blocks = []
    for k in range(4):
        side = slice((k // 2) * some, (k // 2 + 1) * some)
        bus = (iota((some, 2 * near), 1) & (near - 1)) + (k % 2) * near + dev * buses
        blocks.append(incidence(bus, link0[side], link1[side]))
    ct[...] = jnp.concatenate(blocks, axis=0).astype(BF16)
    zcols = [to_column(imp_ref[ij // 3, ij % 3 : ij % 3 + 1, :]) for ij in range(9)]
    for ij in range(9):
        wide = jnp.broadcast_to(zcols[ij], (buses, cases))
        zpack[ij] = jnp.where(lower(wide[:near]), wide[:near], wide[near:])
    inputs[2].wait()

    @pl.loop(0, STEPS)
    def _(step):
        for i in range(3):
            for h, half in enumerate(pack(src[step, i])):
                spack[step, h, i] = half

    def wave_tables():
        first_row, last_row = to_row(first_col), to_row(last_col)
        slot0_col, slot1_col = to_column(slot0_row), to_column(slot1_row)
        seg_sub = iota((segs, lines), 0).astype(F32)
        slot_lane = iota((lines, slots), 1).astype(F32)
        fst = onehot(seg_sub == first_row)
        lst = onehot(seg_sub == last_row)
        gbt[...] = jnp.dot(
            fst, onehot(slot_lane == slot0_col), preferred_element_type=F32
        ).astype(BF16)
        gft[...] = jnp.dot(
            lst, onehot(slot_lane == slot1_col), preferred_element_type=F32
        ).astype(BF16)
        not_first = 1.0 - jnp.sum(fst.astype(F32), axis=1, keepdims=True)
        not_last = 1.0 - jnp.sum(lst.astype(F32), axis=1, keepdims=True)
        for m in range(3):
            r = to_column(refl_ref[m : m + 1, :])
            r_next = pltpu.roll(jnp.broadcast_to(r, (segs, cases)), segs - 1, 0)
            keep_f[m] = jnp.broadcast_to((1.0 - r) * not_first, (segs, cases))
            take_f[m] = jnp.broadcast_to(r * not_first, (segs, cases))
            keep_b[m] = (1.0 - r_next) * not_last
            take_b[m] = r_next * not_last
        single = jnp.where(counts_row == 1.0, 1.0, 0.0)
        a, b = q0.astype(F32) * single, q1.astype(F32) * single
        across = (((1,), (1,)), ((), ()))
        swaps = lax.dot_general(a.astype(BF16), q1, across, preferred_element_type=F32)
        swaps = swaps + lax.dot_general(b.astype(BF16), q0, across, preferred_element_type=F32)
        swaps = swaps.astype(BF16)
        for k in range(4):
            block = swaps[
                (k // 2) * packed : (k // 2 + 1) * packed, (k % 2) * packed : (k % 2 + 1) * packed
            ]
            for w in range(2):
                swap_of[k * packed : (k + 1) * packed, w * packed : (w + 1) * packed] = block

    def advance():
        for m in range(3):
            f, b = fwd[m], bwd[m]
            fwd[m] = keep_f[m] * pltpu.roll(f, 1, 0) + take_f[m] * b
            bwd[m] = keep_b[m] * pltpu.roll(b, segs - 1, 0) + take_b[m] * f

    def scatter(m):
        value = unpack(out[0, m], out[1, m])
        fwd[m] += pick(gbt[...], value)
        bwd[m] += pick(gft[...], value)

    def form_links():
        wait(imp_all, devs - 1, imp_sem.at[1])
        for d in range(devs):
            for i in range(3):
                zrow[3 * i : 3 * i + 3, d * buses : (d + 1) * buses] = imp_all[d, i]
        c = incidence(iota((links, devs * buses), 1), link0, link1)
        c_exact = c.astype(BF16)
        eye = iota((links, links), 0) == iota((links, links), 1)
        for i in range(3):
            for j in range(i + 1):
                z = zrow[3 * i + j : 3 * i + j + 1, :]
                high = z.astype(BF16).astype(F32)
                mid = (z - high).astype(BF16).astype(F32)
                terms = jnp.concatenate([c * high, c * mid, c * (z - high - mid)], axis=0)
                terms = lax.dot_general(
                    terms.astype(BF16), c_exact, (((1,), (1,)), ((), ())), preferred_element_type=F32
                )
                block = terms[:links] + terms[links : 2 * links] + terms[2 * links :]
                if i == j:
                    block = block + jnp.where(eye, resist_ref[...], 0.0)
                for a, b in ((i, j), (j, i))[: 1 + (i != j)]:
                    for k, part in enumerate((near_inv, cross, cross_back, far_inv)):
                        part[a * some : (a + 1) * some, b * some : (b + 1) * some] = block[
                            (k // 2) * some : (k // 2 + 1) * some,
                            (k % 2) * some : (k % 2 + 1) * some,
                        ]

    order = 3 * some
    lane = iota((order, order), 1)

    def eliminate(minv):
        @pl.loop(0, some)
        def _(n):
            spots = [n + w * some for w in range(3)]
            a = minv[...]
            lines_ = [minv[pl.ds(k, 1), :] for k in spots]
            here = [lane == k for k in spots]
            edge = [lane[:1] == k for k in spots]
            cols = [jnp.sum(jnp.where(g, a, 0.0), axis=1, keepdims=True) for g in here]
            block = [
                [jnp.sum(jnp.where(g, r, 0.0), axis=1, keepdims=True) for g in edge]
                for r in lines_
            ]
            for v in range(3):
                inverse = 1.0 / block[v][v]
                row, col = lines_[v], cols[v] * inverse
                a = a - col * row
                scaled = row * inverse
                factor = [block[w][v] for w in range(3)]
                across = [block[v][w] * inverse for w in range(3)]
                for w in range(3):
                    lines_[w] = scaled if w == v else lines_[w] - factor[w] * scaled
                    cols[w] = col if w == v else cols[w] - block[v][w] * col
                for w in range(3):
                    for x in range(3):
                        if w != v and x != v:
                            block[w][x] = block[w][x] - factor[w] * across[x]
                for w in range(3):
                    if w != v:
                        block[w][v], block[v][w] = factor[w] * inverse, across[w]
                block[v][v] = -inverse
            for w in range(3):
                a = jnp.where(here[w], cols[w], a)
                for x in range(3):
                    lines_[w] = jnp.where(edge[x], block[w][x], lines_[w])
            minv[...] = a
            for w in range(3):
                minv[pl.ds(spots[w], 1), :] = lines_[w]

    def exact_dot(a, b):
        return jnp.dot(a, b, precision=EXACT, preferred_element_type=F32)

    def reduce_far():
        ahead[...] = exact_dot(near_inv[...], cross[...])
        far_inv[...] += exact_dot(cross_back[...], ahead[...])

    def link_effect():
        back = exact_dot(cross_back[...], near_inv[...])
        corner = exact_dot(ahead[...], far_inv[...])
        parts = (
            (0, 0, near_inv[...] + exact_dot(corner, back)),
            (0, 1, corner),
            (1, 0, exact_dot(far_inv[...], back)),
            (1, 1, far_inv[...]),
        )
        inverse[...] = jnp.zeros_like(inverse)
        for a, b, part in parts:
            for k in range(3):
                inverse[
                    k, a * some : (a + 1) * some, b * cases : b * cases + 3 * some
                ] = part[k * some : (k + 1) * some]
        c = incidence(iota((buses, links), 0) + dev * buses, link0_row, link1_row)
        drops = [exact_dot(c, inverse[k]) for k in range(3)]
        for i in range(3):
            effect = zcols[3 * i] * drops[0] + zcols[3 * i + 1] * drops[1]
            effect = effect + zcols[3 * i + 2] * drops[2]
            for w, part in enumerate(high_low(effect)):
                for k in range(4):
                    spot = (4 * w + k) * 3 * near + i * near
                    u[spot : spot + near, :] = part[
                        (k // 2) * near : (k // 2 + 1) * near,
                        (k % 2) * cases : (k % 2) * cases + 3 * some,
                    ]

    def apply(values):
        return [
            zpack[3 * i] * values[0] + zpack[3 * i + 1] * values[1] + zpack[3 * i + 2] * values[2]
            for i in range(3)
        ]

    def share(step, h):
        wait(h_recv.at[step, h], total - 1, recv_sem.at[0, step, h])
        parts = [h_recv[step, h, :, i].reshape(packed, cases) for i in range(3)]
        total_in = packed_dot(rsum[...], parts)
        volts = apply([spack[step, h, i] + total_in[i] for i in range(3)])
        for i in range(3):
            open_volts[h, i] = volts[i]
        opened = packed_dot(ct[...], volts)
        for i in range(3):
            e_recv[step, h, dev, i * some : (i + 1) * some, :] = opened[i]

        @pl.loop(1, devs, unroll=devs <= 8)
        def _(p):
            pltpu.make_async_remote_copy(
                src_ref=e_recv.at[step, h, dev],
                dst_ref=e_recv.at[step, h, dev],
                send_sem=send_sem.at[1, step, h],
                recv_sem=recv_sem.at[1, step, h],
                device_id=(area, lax.rem(dev + p, devs)),
                device_id_type=MESH,
            ).start()

    def settle(step, h):
        wait(e_recv.at[step, h], devs - 1, recv_sem.at[1, step, h])
        opened = jnp.sum(e_recv[step, h], axis=0)
        result = jnp.dot(
            u[...], jnp.concatenate(high_low(opened), axis=1), preferred_element_type=F32
        )
        main = 12 * near
        change = fold(result[:main, :cases] + result[:main, cases:] + result[main:, :cases])
        volts = [open_volts[h, i] + change[i * near : (i + 1) * near] for i in range(3)]
        half = cases // 2
        mine = slice(h * half, (h + 1) * half)
        for i in range(3):
            turned = swap(volts[i])
            low, high = (volts[i], turned) if h == 0 else (turned, volts[i])
            volt[step, i, :near, mine] = low[:, mine]
            volt[step, i, near:, mine] = high[:, mine]
        sent = packed_dot(rback[...], volts)
        for i in range(3):
            v_send[step, h, :, i] = sent[i].reshape(total, few, cases)
        push_all(v_send, v_recv, 2, step, h)

    def leave(step, h):
        wait(v_recv.at[step, h], total - 1, recv_sem.at[2, step, h])
        ends = [v_recv[step, h, :, i].reshape(packed, cases) for i in range(3)]
        results = []
        for m in range(3):
            value = trans_ref[m, 0] * ends[0] + trans_ref[m, 1] * ends[1] + trans_ref[m, 2] * ends[2]
            value = value - arr[h, m]
            out[h, m] = value
            results.append(value)
        return results

    def volt_copy(step):
        return pltpu.make_async_copy(volt.at[step], volt_out.at[step], out_sem.at[step])

    form_links()
    eliminate(near_inv)
    for h in range(HALVES):
        share(0, h)
    reduce_far()
    eliminate(far_inv)
    link_effect()
    for h in range(HALVES):
        settle(0, h)
    volt_copy(0).start()
    wave_tables()
    advance()
    gather(nxt)

    @pl.loop(1, STEPS)
    def _(step):
        for h in range(HALVES):
            moved = packed_dot(swap_of[...], leave(step - 1, h))
            for m in range(3):
                arr[h, m] = nxt[h, m] + moved[m]
            inject(step, h)
            push_all(h_send, h_recv, 0, step, h)
        for m in range(3):
            scatter(m)
        advance()

        @pl.when(step < STEPS - 1)
        def _():
            gather(nxt)

        for h in range(HALVES):
            share(step, h)
        for h in range(HALVES):
            settle(step, h)
        volt_copy(step).start()

    for h in range(HALVES):
        leave(STEPS - 1, h)
    outputs = []
    for m in range(3):
        scatter(m)
        for k, (a, b) in enumerate(((fwd, fwd_out), (bwd, bwd_out))):
            outputs.append(
                pltpu.make_async_copy(a.at[m], b.at[m], out_sem.at[STEPS + 2 * m + k])
            )
            outputs[-1].start()

    wait(imp_all, devs - 1, imp_sem.at[0])

    @pl.loop(0, STEPS)
    def _(step):
        volt_copy(step).wait()
        for h in range(HALVES):
            wait(h_send.at[step, h], total - 1, send_sem.at[0, step, h])
            wait(e_recv.at[step, h], devs - 1, send_sem.at[1, step, h])
            wait(v_send.at[step, h], total - 1, send_sem.at[2, step, h])

    for copy in outputs:
        copy.wait()


def hand_over(volt_in, fwd_in, bwd_in, volt_out, fwd_out, bwd_out, volt, fwd, bwd, sems):
    groups = ((fwd_in, fwd, fwd_out), (bwd_in, bwd, bwd_out), (volt_in, volt, volt_out))
    copies = [
        (
            pltpu.make_async_copy(a.at[n], b.at[n], sems.at[0, k, n]),
            pltpu.make_async_copy(b.at[n], c.at[n], sems.at[1, k, n]),
        )
        for k, (a, b, c) in enumerate(groups)
        for n in range(a.shape[0])
    ]
    for first, _ in copies:
        first.start()
    for first, second in copies:
        first.wait()
        second.start()
    for _, second in copies:
        second.wait()


def on_device(
    areas,
    devs,
    wave_fwd,
    wave_bwd,
    seg_reflect,
    seg_count,
    modal_admit,
    modal_transform,
    end_slot,
    recv_bus,
    bus_impedance,
    link_bus,
    link_resist,
    source_current,
):
    total = areas * devs
    cases, segs = wave_fwd.shape[2], wave_fwd.shape[1]
    cap = recv_bus.shape[1] // total
    rows = -(-cap // 8) * 8
    if rows != cap:
        end_slot = end_slot // cap * rows + end_slot % cap
        recv_bus = jnp.pad(
            recv_bus.reshape(total, cap), ((0, 0), (0, rows - cap)), constant_values=-1
        ).reshape(1, total * rows)
    slots = total * rows
    buses = bus_impedance.shape[2]
    links = link_bus.shape[0]
    vmem = pl.BlockSpec(memory_space=pltpu.VMEM)
    smem = pl.BlockSpec(memory_space=pltpu.SMEM)
    anywhere = pl.BlockSpec(memory_space=pl.ANY)
    volt_shape = (STEPS, 3, buses, cases)
    sent = (STEPS, HALVES, total, 3, rows // 2, cases)
    half_slots = (HALVES, 3, slots // 2, cases)
    results = pl.pallas_call(
        functools.partial(kernel, areas, devs),
        out_shape=(
            jax.ShapeDtypeStruct(volt_shape, F32),
            jax.ShapeDtypeStruct(wave_fwd.shape, F32),
            jax.ShapeDtypeStruct(wave_bwd.shape, F32),
        ),
        in_specs=[anywhere] * 2 + [vmem] * 3 + [smem] + [vmem] * 5 + [anywhere],
        out_specs=(anywhere, anywhere, anywhere),
        scratch_shapes=[
            pltpu.VMEM(wave_fwd.shape, F32),
            pltpu.VMEM(wave_bwd.shape, F32),
            pltpu.VMEM(volt_shape, F32),
            pltpu.VMEM(volt_shape, F32),
            pltpu.VMEM(sent, F32),
            pltpu.VMEM(sent, F32),
            pltpu.VMEM((STEPS, HALVES, devs, 3 * links // 2, cases), F32),
            pltpu.VMEM(sent, F32),
            pltpu.VMEM(sent, F32),
            pltpu.VMEM((devs, 3, 3, buses), F32),
            pltpu.VMEM((16, devs * buses), F32),
            pltpu.VMEM((slots, 2 * segs), BF16),
            pltpu.VMEM((2 * slots, slots), BF16),
            pltpu.VMEM((segs, slots), BF16),
            pltpu.VMEM((segs, slots), BF16),
            pltpu.VMEM((2 * buses, slots), BF16),
            pltpu.VMEM((2 * slots, buses), BF16),
            pltpu.VMEM((2 * links, buses), BF16),
            pltpu.VMEM((12 * buses, 3 * links // 2), BF16),
            pltpu.VMEM((3, slots // 2, cases), F32),
            pltpu.VMEM((9, buses // 2, cases), F32),
            pltpu.VMEM((STEPS, HALVES, 3, buses // 2, cases), F32),
            pltpu.VMEM((3, segs, cases), F32),
            pltpu.VMEM((3, segs, cases), F32),
            pltpu.VMEM((3, segs, cases), F32),
            pltpu.VMEM((3, segs, cases), F32),
            pltpu.VMEM(half_slots, F32),
            pltpu.VMEM(half_slots, F32),
            pltpu.VMEM(half_slots, F32),
            pltpu.VMEM((HALVES, 3, buses // 2, cases), F32),
            *[pltpu.VMEM((3 * links // 2, 3 * links // 2), F32)] * 5,
            pltpu.VMEM((3, links, 2 * cases), F32),
            pltpu.SemaphoreType.DMA((3, STEPS, HALVES)),
            pltpu.SemaphoreType.DMA((3, STEPS, HALVES)),
            pltpu.SemaphoreType.DMA((2,)),
            pltpu.SemaphoreType.DMA((3,)),
            pltpu.SemaphoreType.DMA((STEPS + 6,)),
        ],
        compiler_params=pltpu.CompilerParams(
            collective_id=0, has_side_effects=True, vmem_limit_bytes=60 * 1024 * 1024
        ),
        name="transient",
    )(
        wave_fwd,
        wave_bwd,
        seg_reflect,
        seg_count,
        modal_admit,
        modal_transform,
        end_slot.T,
        recv_bus,
        bus_impedance,
        link_bus.T,
        link_resist.reshape(1, links),
        jnp.transpose(source_current, (0, 2, 1, 3)),
    )
    volts, fwd, bwd = pl.pallas_call(
        hand_over,
        out_shape=tuple(jax.ShapeDtypeStruct(a.shape, F32) for a in results),
        in_specs=[anywhere] * 3,
        out_specs=(anywhere,) * 3,
        scratch_shapes=[pltpu.VMEM(a.shape, F32) for a in results]
        + [pltpu.SemaphoreType.DMA((2, 3, STEPS))],
        name="hand_over",
    )(*results)
    return (jnp.transpose(volts, (0, 2, 1, 3)), fwd, bwd)


def solution(mesh):
    in_specs = (
        P(None, ("area", "dev"), None),
        P(None, ("area", "dev"), None),
        P(None, ("area", "dev")),
        P(("area", "dev"), None),
        P(None, ("area", "dev")),
        P(),
        P(("area", "dev"), None),
        P(("area", "dev"), None),
        P(None, None, ("area", "dev")),
        P("area", None),
        P("area"),
        P(None, ("area", "dev"), None, None),
    )
    out_specs = (
        P(None, ("area", "dev"), None, None),
        P(None, ("area", "dev"), None),
        P(None, ("area", "dev"), None),
    )
    return jax.shard_map(
        functools.partial(on_device, mesh.shape["area"], mesh.shape["dev"]),
        mesh=mesh,
        in_specs=in_specs,
        out_specs=out_specs,
        check_vma=False,
    )
```

```python
import functools

import jax
import jax.numpy as jnp
from jax import lax
from jax.experimental import pallas as pl
from jax.experimental.pallas import tpu as pltpu
from jax.sharding import PartitionSpec as P

STEPS = 4
HALVES = 2
MESH = pl.DeviceIdType.MESH
F32 = jnp.float32
BF16 = jnp.bfloat16
EXACT = lax.Precision.HIGHEST


def iota(shape, dim):
    return lax.broadcasted_iota(jnp.int32, shape, dim)


def to_column(row):
    n = row.shape[1]
    eye = iota((n, n), 0) == iota((n, n), 1)
    return jnp.sum(jnp.where(eye, row, 0.0), axis=1, keepdims=True)


def to_row(column):
    n = column.shape[0]
    eye = iota((n, n), 0) == iota((n, n), 1)
    return jnp.sum(jnp.where(eye, column, 0.0), axis=0, keepdims=True)


def onehot(flag):
    return jnp.where(flag, 1.0, 0.0).astype(BF16)


def high_low(value):
    high = value.astype(BF16)
    return high, (value - high.astype(F32)).astype(BF16)


def pick(matrix, value):
    n = value.shape[1]
    both = jnp.dot(
        matrix, jnp.concatenate(high_low(value), axis=1), preferred_element_type=F32
    )
    return both[:, :n] + both[:, n:]


def swap(value):
    return pltpu.roll(value, value.shape[1] // 2, 1)


def lower(value):
    return iota(value.shape, 1) < value.shape[1] // 2


def pack(value):
    n = value.shape[0] // 2
    top, bottom = value[:n], value[n:]
    left = lower(top)
    return jnp.where(left, top, swap(bottom)), jnp.where(left, swap(top), bottom)


def unpack(first, second):
    left = lower(first)
    return jnp.concatenate(
        [jnp.where(left, first, swap(second)), jnp.where(left, swap(first), second)], axis=0
    )


def fold(result):
    m = result.shape[0] // 4
    tl, tr, bl, br = (result[k * m : (k + 1) * m] for k in range(4))
    left = lower(tl)
    return jnp.where(left, tl, br) + swap(jnp.where(left, bl, tr))


def packed_dot(table, parts):
    n = parts[0].shape[1]
    both = jnp.concatenate(high_low(jnp.concatenate(parts, axis=1)), axis=0)
    result = jnp.dot(table, both, preferred_element_type=F32)
    return [fold(result[:, k * n : (k + 1) * n]) for k in range(len(parts))]


def kernel(
    areas,
    devs,
    fwd_in,
    bwd_in,
    refl_ref,
    count_ref,
    admit_ref,
    trans_ref,
    slot_ref,
    recv_ref,
    imp_ref,
    link_ref,
    resist_ref,
    src_in,
    volt_out,
    fwd_out,
    bwd_out,
    fwd,
    bwd,
    src,
    volt,
    h_send,
    h_recv,
    e_recv,
    e_pair,
    v_send,
    v_recv,
    imp_all,
    zrow,
    ends_of,
    swap_of,
    gbt,
    gft,
    rsum,
    rback,
    ct,
    u,
    adm,
    zpack,
    spack,
    keep_f,
    take_f,
    keep_b,
    take_b,
    arr,
    nxt,
    out,
    open_volts,
    near_inv,
    cross,
    cross_back,
    far_inv,
    ahead,
    inverse,
    send_sem,
    recv_sem,
    imp_sem,
    in_sem,
    out_sem,
):
    total = areas * devs
    area, dev = lax.axis_index("area"), lax.axis_index("dev")
    me = area * devs + dev
    cases = fwd.shape[2]
    segs = fwd.shape[1]
    lines = slot_ref.shape[1]
    slots = recv_ref.shape[1]
    buses = imp_ref.shape[2]
    links = link_ref.shape[1]
    rows = slots // total
    few = rows // 2
    packed = slots // 2
    near = buses // 2
    some = links // 2

    inputs = [
        pltpu.make_async_copy(a, b, in_sem.at[k])
        for k, (a, b) in enumerate(((fwd_in, fwd), (bwd_in, bwd), (src_in, src)))
    ]
    for copy in inputs:
        copy.start()

    barrier = pltpu.get_barrier_semaphore()

    def peer_of(p):
        other_area = area ^ (areas - 1 - lax.rem(p, areas))
        other_dev = dev ^ (devs - 1 - p // areas)
        return other_area * devs + other_dev, (other_area, other_dev)

    def turned_of(p):
        peer = lax.rem(me + p + 1, total)
        return peer, (peer // devs, lax.rem(peer, devs))

    @pl.loop(0, total - 1)
    def _(p):
        _, where = peer_of(p)
        pl.semaphore_signal(barrier, inc=1, device_id=where, device_id_type=MESH)

    def push_all(send, recv, phase, step, h):
        @pl.loop(0, total - 1, unroll=total <= 32)
        def _(p):
            peer, where = turned_of(p) if phase == 2 else peer_of(p)
            pltpu.make_async_remote_copy(
                src_ref=send.at[step, h, peer],
                dst_ref=recv.at[step, h, me],
                send_sem=send_sem.at[phase, step, h],
                recv_sem=recv_sem.at[phase, step, h],
                device_id=where,
                device_id_type=MESH,
            ).start()

        recv[step, h, me] = send[step, h, me]

    def wait(buf, count, sem):
        ref = buf.at[pl.ds(0, count)]
        pltpu.make_async_copy(ref, ref, sem).wait()

    def place(slot):
        bits = few.bit_length() - 1
        upper = lax.shift_right_logical(slot, bits)
        return (upper & 1) * packed + lax.shift_right_logical(upper, 1) * few + (slot & (few - 1))

    counts_row = count_ref[...].astype(F32)
    counts_col = to_column(counts_row)
    square = (lines, lines)
    first_col = jnp.sum(
        jnp.where(iota(square, 1) < iota(square, 0), counts_row, 0.0), axis=1, keepdims=True
    )
    last_col = first_col + counts_col - 1.0
    slot0_row = place(slot_ref[0:1, :]).astype(F32)
    slot1_row = place(slot_ref[1:2, :]).astype(F32)
    seg_lane = iota((lines, segs), 1).astype(F32)
    slot_sub = iota((slots, lines), 0).astype(F32)
    q0, q1 = onehot(slot_sub == slot0_row), onehot(slot_sub == slot1_row)
    ends_of[:, :segs] = jnp.dot(
        q0, onehot(seg_lane == first_col), preferred_element_type=F32
    ).astype(BF16)
    ends_of[:, segs:] = jnp.dot(
        q1, onehot(seg_lane == last_col), preferred_element_type=F32
    ).astype(BF16)
    held = q0.astype(F32) + q1.astype(F32)
    for m in range(3):
        column = 2.0 * jnp.sum(held * admit_ref[m : m + 1, :], axis=1, keepdims=True)
        wide = jnp.broadcast_to(column, (slots, cases))
        adm[m] = jnp.where(lower(wide[:packed]), wide[:packed], wide[packed:])

    def gather(target):
        for m in range(3):
            both = jnp.concatenate([bwd[m], fwd[m]], axis=0)
            for h, half in enumerate(pack(pick(ends_of[...], both))):
                target[h, m] = half

    def inject(step, h):
        for i in range(3):
            value = trans_ref[0, i] * (adm[0] * arr[h, 0])
            value = value + trans_ref[1, i] * (adm[1] * arr[h, 1])
            value = value + trans_ref[2, i] * (adm[2] * arr[h, 2])
            h_send[step, h, :, i] = value.reshape(total, few, cases)

    inputs[0].wait()
    inputs[1].wait()
    gather(arr)
    for h in range(HALVES):
        inject(0, h)
    pl.semaphore_wait(barrier, total - 1)

    @pl.loop(1, devs)
    def _(p):
        other = lax.rem(dev + p, devs)
        pltpu.make_async_remote_copy(
            src_ref=imp_ref,
            dst_ref=imp_all.at[dev],
            send_sem=imp_sem.at[0],
            recv_sem=imp_sem.at[1],
            device_id=(area, other),
            device_id_type=MESH,
        ).start()

    for h in range(HALVES):
        push_all(h_send, h_recv, 0, 0, h)
    imp_all[dev] = imp_ref[...]

    recv_placed = jnp.where(
        iota((slots, slots), 0) == place(iota((slots, slots), 1)), recv_ref[...].astype(F32), 0.0
    )
    recv_col = jnp.sum(recv_placed, axis=1, keepdims=True)
    recv_row = to_row(recv_col)
    for k in range(4):
        side = slice((k % 2) * packed, (k % 2 + 1) * packed)
        bus = (iota((near, packed), 0) + (k // 2) * near).astype(F32)
        block = onehot(bus == recv_row[:, side])
        for w in range(2):
            rsum[k * near : (k + 1) * near, w * packed : (w + 1) * packed] = block
        side = slice((k // 2) * packed, (k // 2 + 1) * packed)
        bus = ((iota((packed, 2 * near), 1) & (near - 1)) + (k % 2) * near).astype(F32)
        rback[k * packed : (k + 1) * packed, :] = onehot(bus == recv_col[side])

    link0_row, link1_row = link_ref[0:1, :].astype(F32), link_ref[1:2, :].astype(F32)
    link0, link1 = to_column(link0_row), to_column(link1_row)

    def incidence(index, a, b):
        index = index.astype(F32)
        return jnp.where(index == a, 1.0, 0.0) - jnp.where(index == b, 1.0, 0.0)

    blocks = []
    for k in range(4):
        side = slice((k // 2) * some, (k // 2 + 1) * some)
        bus = (iota((some, 2 * near), 1) & (near - 1)) + (k % 2) * near + dev * buses
        blocks.append(incidence(bus, link0[side], link1[side]))
    ct[...] = jnp.concatenate(blocks, axis=0).astype(BF16)
    zcols = [to_column(imp_ref[ij // 3, ij % 3 : ij % 3 + 1, :]) for ij in range(9)]
    for ij in range(9):
        wide = jnp.broadcast_to(zcols[ij], (buses, cases))
        zpack[ij] = jnp.where(lower(wide[:near]), wide[:near], wide[near:])
    inputs[2].wait()

    @pl.loop(0, STEPS)
    def _(step):
        for i in range(3):
            for h, half in enumerate(pack(src[step, i])):
                spack[step, h, i] = half

    def wave_tables():
        first_row, last_row = to_row(first_col), to_row(last_col)
        slot0_col, slot1_col = to_column(slot0_row), to_column(slot1_row)
        seg_sub = iota((segs, lines), 0).astype(F32)
        slot_lane = iota((lines, slots), 1).astype(F32)
        fst = onehot(seg_sub == first_row)
        lst = onehot(seg_sub == last_row)
        gbt[...] = jnp.dot(
            fst, onehot(slot_lane == slot0_col), preferred_element_type=F32
        ).astype(BF16)
        gft[...] = jnp.dot(
            lst, onehot(slot_lane == slot1_col), preferred_element_type=F32
        ).astype(BF16)
        not_first = 1.0 - jnp.sum(fst.astype(F32), axis=1, keepdims=True)
        not_last = 1.0 - jnp.sum(lst.astype(F32), axis=1, keepdims=True)
        for m in range(3):
            r = to_column(refl_ref[m : m + 1, :])
            r_next = pltpu.roll(jnp.broadcast_to(r, (segs, cases)), segs - 1, 0)
            keep_f[m] = jnp.broadcast_to((1.0 - r) * not_first, (segs, cases))
            take_f[m] = jnp.broadcast_to(r * not_first, (segs, cases))
            keep_b[m] = (1.0 - r_next) * not_last
            take_b[m] = r_next * not_last
        single = jnp.where(counts_row == 1.0, 1.0, 0.0)
        a, b = q0.astype(F32) * single, q1.astype(F32) * single
        across = (((1,), (1,)), ((), ()))
        swaps = lax.dot_general(a.astype(BF16), q1, across, preferred_element_type=F32)
        swaps = swaps + lax.dot_general(b.astype(BF16), q0, across, preferred_element_type=F32)
        swaps = swaps.astype(BF16)
        for k in range(4):
            block = swaps[
                (k // 2) * packed : (k // 2 + 1) * packed, (k % 2) * packed : (k % 2 + 1) * packed
            ]
            for w in range(2):
                swap_of[k * packed : (k + 1) * packed, w * packed : (w + 1) * packed] = block

    def advance():
        for m in range(3):
            f, b = fwd[m], bwd[m]
            fwd[m] = keep_f[m] * pltpu.roll(f, 1, 0) + take_f[m] * b
            bwd[m] = keep_b[m] * pltpu.roll(b, segs - 1, 0) + take_b[m] * f

    def scatter(m):
        value = unpack(out[0, m], out[1, m])
        fwd[m] += pick(gbt[...], value)
        bwd[m] += pick(gft[...], value)

    def form_links():
        wait(imp_all, devs - 1, imp_sem.at[1])
        for d in range(devs):
            for i in range(3):
                zrow[3 * i : 3 * i + 3, d * buses : (d + 1) * buses] = imp_all[d, i]
        c = incidence(iota((links, devs * buses), 1), link0, link1)
        c_exact = c.astype(BF16)
        eye = iota((links, links), 0) == iota((links, links), 1)
        for i in range(3):
            for j in range(i + 1):
                z = zrow[3 * i + j : 3 * i + j + 1, :]
                high = z.astype(BF16).astype(F32)
                mid = (z - high).astype(BF16).astype(F32)
                terms = jnp.concatenate([c * high, c * mid, c * (z - high - mid)], axis=0)
                terms = lax.dot_general(
                    terms.astype(BF16), c_exact, (((1,), (1,)), ((), ())), preferred_element_type=F32
                )
                block = terms[:links] + terms[links : 2 * links] + terms[2 * links :]
                if i == j:
                    block = block + jnp.where(eye, resist_ref[...], 0.0)
                for a, b in ((i, j), (j, i))[: 1 + (i != j)]:
                    for k, part in enumerate((near_inv, cross, cross_back, far_inv)):
                        part[a * some : (a + 1) * some, b * some : (b + 1) * some] = block[
                            (k // 2) * some : (k // 2 + 1) * some,
                            (k % 2) * some : (k % 2 + 1) * some,
                        ]

    order = 3 * some
    lane = iota((order, order), 1)

    def eliminate(minv):
        @pl.loop(0, some)
        def _(n):
            spots = [n + w * some for w in range(3)]
            a = minv[...]
            lines_ = [minv[pl.ds(k, 1), :] for k in spots]
            here = [lane == k for k in spots]
            edge = [lane[:1] == k for k in spots]
            cols = [jnp.sum(jnp.where(g, a, 0.0), axis=1, keepdims=True) for g in here]
            block = [
                [jnp.sum(jnp.where(g, r, 0.0), axis=1, keepdims=True) for g in edge]
                for r in lines_
            ]
            for v in range(3):
                inverse = 1.0 / block[v][v]
                row, col = lines_[v], cols[v] * inverse
                a = a - col * row
                scaled = row * inverse
                factor = [block[w][v] for w in range(3)]
                across = [block[v][w] * inverse for w in range(3)]
                for w in range(3):
                    lines_[w] = scaled if w == v else lines_[w] - factor[w] * scaled
                    cols[w] = col if w == v else cols[w] - block[v][w] * col
                for w in range(3):
                    for x in range(3):
                        if w != v and x != v:
                            block[w][x] = block[w][x] - factor[w] * across[x]
                for w in range(3):
                    if w != v:
                        block[w][v], block[v][w] = factor[w] * inverse, across[w]
                block[v][v] = -inverse
            for w in range(3):
                a = jnp.where(here[w], cols[w], a)
                for x in range(3):
                    lines_[w] = jnp.where(edge[x], block[w][x], lines_[w])
            minv[...] = a
            for w in range(3):
                minv[pl.ds(spots[w], 1), :] = lines_[w]

    def exact_dot(a, b):
        return jnp.dot(a, b, precision=EXACT, preferred_element_type=F32)

    def reduce_far():
        ahead[...] = exact_dot(near_inv[...], cross[...])
        far_inv[...] += exact_dot(cross_back[...], ahead[...])

    def link_effect():
        back = exact_dot(cross_back[...], near_inv[...])
        corner = exact_dot(ahead[...], far_inv[...])
        parts = (
            (0, 0, near_inv[...] + exact_dot(corner, back)),
            (0, 1, corner),
            (1, 0, exact_dot(far_inv[...], back)),
            (1, 1, far_inv[...]),
        )
        inverse[...] = jnp.zeros_like(inverse)
        for a, b, part in parts:
            for k in range(3):
                inverse[
                    k, a * some : (a + 1) * some, b * cases : b * cases + 3 * some
                ] = part[k * some : (k + 1) * some]
        c = incidence(iota((buses, links), 0) + dev * buses, link0_row, link1_row)
        drops = [exact_dot(c, inverse[k]) for k in range(3)]
        for i in range(3):
            effect = zcols[3 * i] * drops[0] + zcols[3 * i + 1] * drops[1]
            effect = effect + zcols[3 * i + 2] * drops[2]
            for w, part in enumerate(high_low(effect)):
                for k in range(4):
                    spot = (4 * w + k) * 3 * near + i * near
                    u[spot : spot + near, :] = part[
                        (k // 2) * near : (k // 2 + 1) * near,
                        (k % 2) * cases : (k % 2) * cases + 3 * some,
                    ]

    def apply(values):
        return [
            zpack[3 * i] * values[0] + zpack[3 * i + 1] * values[1] + zpack[3 * i + 2] * values[2]
            for i in range(3)
        ]

    def share(step, h):
        wait(h_recv.at[step, h], total - 1, recv_sem.at[0, step, h])
        parts = [h_recv[step, h, :, i].reshape(packed, cases) for i in range(3)]
        total_in = packed_dot(rsum[...], parts)
        volts = apply([spack[step, h, i] + total_in[i] for i in range(3)])
        for i in range(3):
            open_volts[h, i] = volts[i]
        opened = packed_dot(ct[...], volts)
        for i in range(3):
            e_recv[step, h, dev // 2, i * some : (i + 1) * some, :] = opened[i]

        @pl.loop(1, devs // 2, unroll=devs <= 8)
        def _(p):
            pltpu.make_async_remote_copy(
                src_ref=e_recv.at[step, h, dev // 2],
                dst_ref=e_recv.at[step, h, dev // 2],
                send_sem=send_sem.at[1, step, h],
                recv_sem=recv_sem.at[1, step, h],
                device_id=(area, dev ^ (devs - 2 * p)),
                device_id_type=MESH,
            ).start()

    def settle(step, h):
        wait(e_recv.at[step, h], devs // 2 - 1, recv_sem.at[1, step, h])
        own = lax.rem(dev, 2)
        e_pair[step, h, own] = jnp.sum(e_recv[step, h], axis=0)
        swap_sum = pltpu.make_async_remote_copy(
            src_ref=e_pair.at[step, h, own],
            dst_ref=e_pair.at[step, h, own],
            send_sem=send_sem.at[3, step, h],
            recv_sem=recv_sem.at[3, step, h],
            device_id=(area, dev ^ 1),
            device_id_type=MESH,
        )
        swap_sum.start()
        swap_sum.wait()
        opened = e_pair[step, h, 0] + e_pair[step, h, 1]
        result = jnp.dot(
            u[...], jnp.concatenate(high_low(opened), axis=1), preferred_element_type=F32
        )
        main = 12 * near
        change = fold(result[:main, :cases] + result[:main, cases:] + result[main:, :cases])
        volts = [open_volts[h, i] + change[i * near : (i + 1) * near] for i in range(3)]
        half = cases // 2
        mine = slice(h * half, (h + 1) * half)
        for i in range(3):
            turned = swap(volts[i])
            low, high = (volts[i], turned) if h == 0 else (turned, volts[i])
            volt[step, i, :near, mine] = low[:, mine]
            volt[step, i, near:, mine] = high[:, mine]
        sent = packed_dot(rback[...], volts)
        for i in range(3):
            v_send[step, h, :, i] = sent[i].reshape(total, few, cases)
        push_all(v_send, v_recv, 2, step, h)

    def leave(step, h):
        wait(v_recv.at[step, h], total - 1, recv_sem.at[2, step, h])
        ends = [v_recv[step, h, :, i].reshape(packed, cases) for i in range(3)]
        results = []
        for m in range(3):
            value = trans_ref[m, 0] * ends[0] + trans_ref[m, 1] * ends[1] + trans_ref[m, 2] * ends[2]
            value = value - arr[h, m]
            out[h, m] = value
            results.append(value)
        return results

    def volt_copy(step):
        return pltpu.make_async_copy(volt.at[step], volt_out.at[step], out_sem.at[step])

    form_links()
    eliminate(near_inv)
    share(0, 0)
    reduce_far()
    share(0, 1)
    eliminate(far_inv)
    link_effect()
    for h in range(HALVES):
        settle(0, h)
    volt_copy(0).start()
    wave_tables()
    advance()
    gather(nxt)

    @pl.loop(1, STEPS)
    def _(step):
        for h in range(HALVES):
            moved = packed_dot(swap_of[...], leave(step - 1, h))
            for m in range(3):
                arr[h, m] = nxt[h, m] + moved[m]
            inject(step, h)
            push_all(h_send, h_recv, 0, step, h)
        share(step, 0)
        for m in range(3):
            scatter(m)
        advance()

        @pl.when(step < STEPS - 1)
        def _():
            gather(nxt)

        share(step, 1)
        for h in range(HALVES):
            settle(step, h)
        volt_copy(step).start()

    for h in range(HALVES):
        leave(STEPS - 1, h)
    outputs = []
    for m in range(3):
        scatter(m)
        for k, (a, b) in enumerate(((fwd, fwd_out), (bwd, bwd_out))):
            outputs.append(
                pltpu.make_async_copy(a.at[m], b.at[m], out_sem.at[STEPS + 2 * m + k])
            )
            outputs[-1].start()

    wait(imp_all, devs - 1, imp_sem.at[0])

    @pl.loop(0, STEPS)
    def _(step):
        volt_copy(step).wait()
        for h in range(HALVES):
            wait(h_send.at[step, h], total - 1, send_sem.at[0, step, h])
            wait(e_recv.at[step, h], devs // 2 - 1, send_sem.at[1, step, h])
            wait(v_send.at[step, h], total - 1, send_sem.at[2, step, h])

    for copy in outputs:
        copy.wait()


def hand_over(volt_in, fwd_in, bwd_in, volt_out, fwd_out, bwd_out, volt, fwd, bwd, sems):
    groups = ((fwd_in, fwd, fwd_out), (bwd_in, bwd, bwd_out), (volt_in, volt, volt_out))
    copies = [
        (
            pltpu.make_async_copy(a.at[n], b.at[n], sems.at[0, k, n]),
            pltpu.make_async_copy(b.at[n], c.at[n], sems.at[1, k, n]),
        )
        for k, (a, b, c) in enumerate(groups)
        for n in range(a.shape[0])
    ]
    for first, _ in copies:
        first.start()
    for first, second in copies:
        first.wait()
        second.start()
    for _, second in copies:
        second.wait()


def on_device(
    areas,
    devs,
    wave_fwd,
    wave_bwd,
    seg_reflect,
    seg_count,
    modal_admit,
    modal_transform,
    end_slot,
    recv_bus,
    bus_impedance,
    link_bus,
    link_resist,
    source_current,
):
    total = areas * devs
    cases, segs = wave_fwd.shape[2], wave_fwd.shape[1]
    cap = recv_bus.shape[1] // total
    rows = -(-cap // 8) * 8
    if rows != cap:
        end_slot = end_slot // cap * rows + end_slot % cap
        recv_bus = jnp.pad(
            recv_bus.reshape(total, cap), ((0, 0), (0, rows - cap)), constant_values=-1
        ).reshape(1, total * rows)
    slots = total * rows
    buses = bus_impedance.shape[2]
    links = link_bus.shape[0]
    vmem = pl.BlockSpec(memory_space=pltpu.VMEM)
    smem = pl.BlockSpec(memory_space=pltpu.SMEM)
    anywhere = pl.BlockSpec(memory_space=pl.ANY)
    volt_shape = (STEPS, 3, buses, cases)
    sent = (STEPS, HALVES, total, 3, rows // 2, cases)
    half_slots = (HALVES, 3, slots // 2, cases)
    results = pl.pallas_call(
        functools.partial(kernel, areas, devs),
        out_shape=(
            jax.ShapeDtypeStruct(volt_shape, F32),
            jax.ShapeDtypeStruct(wave_fwd.shape, F32),
            jax.ShapeDtypeStruct(wave_bwd.shape, F32),
        ),
        in_specs=[anywhere] * 2 + [vmem] * 3 + [smem] + [vmem] * 5 + [anywhere],
        out_specs=(anywhere, anywhere, anywhere),
        scratch_shapes=[
            pltpu.VMEM(wave_fwd.shape, F32),
            pltpu.VMEM(wave_bwd.shape, F32),
            pltpu.VMEM(volt_shape, F32),
            pltpu.VMEM(volt_shape, F32),
            pltpu.VMEM(sent, F32),
            pltpu.VMEM(sent, F32),
            pltpu.VMEM((STEPS, HALVES, devs // 2, 3 * links // 2, cases), F32),
            pltpu.VMEM((STEPS, HALVES, 2, 3 * links // 2, cases), F32),
            pltpu.VMEM(sent, F32),
            pltpu.VMEM(sent, F32),
            pltpu.VMEM((devs, 3, 3, buses), F32),
            pltpu.VMEM((16, devs * buses), F32),
            pltpu.VMEM((slots, 2 * segs), BF16),
            pltpu.VMEM((2 * slots, slots), BF16),
            pltpu.VMEM((segs, slots), BF16),
            pltpu.VMEM((segs, slots), BF16),
            pltpu.VMEM((2 * buses, slots), BF16),
            pltpu.VMEM((2 * slots, buses), BF16),
            pltpu.VMEM((2 * links, buses), BF16),
            pltpu.VMEM((12 * buses, 3 * links // 2), BF16),
            pltpu.VMEM((3, slots // 2, cases), F32),
            pltpu.VMEM((9, buses // 2, cases), F32),
            pltpu.VMEM((STEPS, HALVES, 3, buses // 2, cases), F32),
            pltpu.VMEM((3, segs, cases), F32),
            pltpu.VMEM((3, segs, cases), F32),
            pltpu.VMEM((3, segs, cases), F32),
            pltpu.VMEM((3, segs, cases), F32),
            pltpu.VMEM(half_slots, F32),
            pltpu.VMEM(half_slots, F32),
            pltpu.VMEM(half_slots, F32),
            pltpu.VMEM((HALVES, 3, buses // 2, cases), F32),
            *[pltpu.VMEM((3 * links // 2, 3 * links // 2), F32)] * 5,
            pltpu.VMEM((3, links, 2 * cases), F32),
            pltpu.SemaphoreType.DMA((4, STEPS, HALVES)),
            pltpu.SemaphoreType.DMA((4, STEPS, HALVES)),
            pltpu.SemaphoreType.DMA((2,)),
            pltpu.SemaphoreType.DMA((3,)),
            pltpu.SemaphoreType.DMA((STEPS + 6,)),
        ],
        compiler_params=pltpu.CompilerParams(
            collective_id=0, has_side_effects=True, vmem_limit_bytes=60 * 1024 * 1024
        ),
        name="transient",
    )(
        wave_fwd,
        wave_bwd,
        seg_reflect,
        seg_count,
        modal_admit,
        modal_transform,
        end_slot.T,
        recv_bus,
        bus_impedance,
        link_bus.T,
        link_resist.reshape(1, links),
        jnp.transpose(source_current, (0, 2, 1, 3)),
    )
    volts, fwd, bwd = pl.pallas_call(
        hand_over,
        out_shape=tuple(jax.ShapeDtypeStruct(a.shape, F32) for a in results),
        in_specs=[anywhere] * 3,
        out_specs=(anywhere,) * 3,
        scratch_shapes=[pltpu.VMEM(a.shape, F32) for a in results]
        + [pltpu.SemaphoreType.DMA((2, 3, STEPS))],
        name="hand_over",
    )(*results)
    return (jnp.transpose(volts, (0, 2, 1, 3)), fwd, bwd)


def solution(mesh):
    in_specs = (
        P(None, ("area", "dev"), None),
        P(None, ("area", "dev"), None),
        P(None, ("area", "dev")),
        P(("area", "dev"), None),
        P(None, ("area", "dev")),
        P(),
        P(("area", "dev"), None),
        P(("area", "dev"), None),
        P(None, None, ("area", "dev")),
        P("area", None),
        P("area"),
        P(None, ("area", "dev"), None, None),
    )
    out_specs = (
        P(None, ("area", "dev"), None, None),
        P(None, ("area", "dev"), None),
        P(None, ("area", "dev"), None),
    )
    return jax.shard_map(
        functools.partial(on_device, mesh.shape["area"], mesh.shape["dev"]),
        mesh=mesh,
        in_specs=in_specs,
        out_specs=out_specs,
        check_vma=False,
    )
```

```python
import functools

import jax
import jax.numpy as jnp
from jax import lax
from jax.experimental import pallas as pl
from jax.experimental.pallas import tpu as pltpu
from jax.sharding import PartitionSpec as P

STEPS = 4
HALVES = 2
MESH = pl.DeviceIdType.MESH
F32 = jnp.float32
BF16 = jnp.bfloat16
EXACT = lax.Precision.HIGHEST


def iota(shape, dim):
    return lax.broadcasted_iota(jnp.int32, shape, dim)


def to_column(row):
    n = row.shape[1]
    eye = iota((n, n), 0) == iota((n, n), 1)
    return jnp.sum(jnp.where(eye, row, 0.0), axis=1, keepdims=True)


def to_row(column):
    n = column.shape[0]
    eye = iota((n, n), 0) == iota((n, n), 1)
    return jnp.sum(jnp.where(eye, column, 0.0), axis=0, keepdims=True)


def onehot(flag):
    return jnp.where(flag, 1.0, 0.0).astype(BF16)


def high_low(value):
    high = value.astype(BF16)
    return high, (value - high.astype(F32)).astype(BF16)


def pick(matrix, value):
    n = value.shape[1]
    both = jnp.dot(
        matrix, jnp.concatenate(high_low(value), axis=1), preferred_element_type=F32
    )
    return both[:, :n] + both[:, n:]


def swap(value):
    return pltpu.roll(value, value.shape[1] // 2, 1)


def lower(value):
    return iota(value.shape, 1) < value.shape[1] // 2


def pack(value):
    n = value.shape[0] // 2
    top, bottom = value[:n], value[n:]
    left = lower(top)
    return jnp.where(left, top, swap(bottom)), jnp.where(left, swap(top), bottom)


def unpack(first, second):
    left = lower(first)
    return jnp.concatenate(
        [jnp.where(left, first, swap(second)), jnp.where(left, swap(first), second)], axis=0
    )


def fold(result):
    m = result.shape[0] // 4
    tl, tr, bl, br = (result[k * m : (k + 1) * m] for k in range(4))
    left = lower(tl)
    return jnp.where(left, tl, br) + swap(jnp.where(left, bl, tr))


def packed_dot(table, parts):
    n = parts[0].shape[1]
    both = jnp.concatenate(high_low(jnp.concatenate(parts, axis=1)), axis=0)
    result = jnp.dot(table, both, preferred_element_type=F32)
    return [fold(result[:, k * n : (k + 1) * n]) for k in range(len(parts))]


def kernel(
    areas,
    devs,
    fwd_in,
    bwd_in,
    refl_ref,
    count_ref,
    admit_ref,
    trans_ref,
    slot_ref,
    recv_ref,
    imp_ref,
    link_ref,
    resist_ref,
    src_in,
    volt_out,
    fwd_out,
    bwd_out,
    fwd,
    bwd,
    src,
    volt,
    h_send,
    h_recv,
    e_recv,
    e_pair,
    v_send,
    v_recv,
    imp_all,
    zrow,
    ends_of,
    swap_of,
    gbt,
    gft,
    rsum,
    rback,
    ct,
    u,
    adm,
    zpack,
    spack,
    keep_f,
    take_f,
    keep_b,
    take_b,
    arr,
    nxt,
    out,
    open_volts,
    near_inv,
    cross,
    cross_back,
    far_inv,
    ahead,
    inverse,
    send_sem,
    recv_sem,
    imp_sem,
    in_sem,
    out_sem,
):
    total = areas * devs
    area, dev = lax.axis_index("area"), lax.axis_index("dev")
    me = area * devs + dev
    cases = fwd.shape[2]
    segs = fwd.shape[1]
    lines = slot_ref.shape[1]
    slots = recv_ref.shape[1]
    buses = imp_ref.shape[2]
    links = link_ref.shape[1]
    rows = slots // total
    few = rows // 2
    packed = slots // 2
    near = buses // 2
    some = links // 2

    inputs = [
        pltpu.make_async_copy(a, b, in_sem.at[k])
        for k, (a, b) in enumerate(((fwd_in, fwd), (bwd_in, bwd), (src_in, src)))
    ]
    for copy in inputs:
        copy.start()

    barrier = pltpu.get_barrier_semaphore()

    def peer_of(p):
        other_area = area ^ (areas - 1 - lax.rem(p, areas))
        other_dev = dev ^ (devs - 1 - p // areas)
        return other_area * devs + other_dev, (other_area, other_dev)

    def turned_of(p):
        peer = lax.rem(me + p + 1, total)
        return peer, (peer // devs, lax.rem(peer, devs))

    @pl.loop(0, total - 1)
    def _(p):
        _, where = peer_of(p)
        pl.semaphore_signal(barrier, inc=1, device_id=where, device_id_type=MESH)

    def push_all(send, recv, phase, step, h):
        @pl.loop(0, total - 1, unroll=total <= 32)
        def _(p):
            peer, where = turned_of(p) if phase == 2 else peer_of(p)
            pltpu.make_async_remote_copy(
                src_ref=send.at[step, h, peer],
                dst_ref=recv.at[step, h, me],
                send_sem=send_sem.at[phase, step, h],
                recv_sem=recv_sem.at[phase, step, h],
                device_id=where,
                device_id_type=MESH,
            ).start()

        recv[step, h, me] = send[step, h, me]

    def wait(buf, count, sem):
        ref = buf.at[pl.ds(0, count)]
        pltpu.make_async_copy(ref, ref, sem).wait()

    def place(slot):
        bits = few.bit_length() - 1
        upper = lax.shift_right_logical(slot, bits)
        return (upper & 1) * packed + lax.shift_right_logical(upper, 1) * few + (slot & (few - 1))

    counts_row = count_ref[...].astype(F32)
    counts_col = to_column(counts_row)
    square = (lines, lines)
    first_col = jnp.sum(
        jnp.where(iota(square, 1) < iota(square, 0), counts_row, 0.0), axis=1, keepdims=True
    )
    last_col = first_col + counts_col - 1.0
    slot0_row = place(slot_ref[0:1, :]).astype(F32)
    slot1_row = place(slot_ref[1:2, :]).astype(F32)
    seg_lane = iota((lines, segs), 1).astype(F32)
    slot_sub = iota((slots, lines), 0).astype(F32)
    q0, q1 = onehot(slot_sub == slot0_row), onehot(slot_sub == slot1_row)
    ends_of[:, :segs] = jnp.dot(
        q0, onehot(seg_lane == first_col), preferred_element_type=F32
    ).astype(BF16)
    ends_of[:, segs:] = jnp.dot(
        q1, onehot(seg_lane == last_col), preferred_element_type=F32
    ).astype(BF16)
    held = q0.astype(F32) + q1.astype(F32)
    for m in range(3):
        column = 2.0 * jnp.sum(held * admit_ref[m : m + 1, :], axis=1, keepdims=True)
        wide = jnp.broadcast_to(column, (slots, cases))
        adm[m] = jnp.where(lower(wide[:packed]), wide[:packed], wide[packed:])

    def gather(target):
        for m in range(3):
            both = jnp.concatenate([bwd[m], fwd[m]], axis=0)
            for h, half in enumerate(pack(pick(ends_of[...], both))):
                target[h, m] = half

    def inject(step, h):
        for i in range(3):
            value = trans_ref[0, i] * (adm[0] * arr[h, 0])
            value = value + trans_ref[1, i] * (adm[1] * arr[h, 1])
            value = value + trans_ref[2, i] * (adm[2] * arr[h, 2])
            h_send[step, h, :, i] = value.reshape(total, few, cases)

    inputs[0].wait()
    inputs[1].wait()
    gather(arr)
    for h in range(HALVES):
        inject(0, h)
    pl.semaphore_wait(barrier, total - 1)

    @pl.loop(1, devs)
    def _(p):
        other = lax.rem(dev + p, devs)
        pltpu.make_async_remote_copy(
            src_ref=imp_ref,
            dst_ref=imp_all.at[dev],
            send_sem=imp_sem.at[0],
            recv_sem=imp_sem.at[1],
            device_id=(area, other),
            device_id_type=MESH,
        ).start()

    for h in range(HALVES):
        push_all(h_send, h_recv, 0, 0, h)
    imp_all[dev] = imp_ref[...]

    recv_placed = jnp.where(
        iota((slots, slots), 0) == place(iota((slots, slots), 1)), recv_ref[...].astype(F32), 0.0
    )
    recv_col = jnp.sum(recv_placed, axis=1, keepdims=True)
    recv_row = to_row(recv_col)
    for k in range(4):
        side = slice((k % 2) * packed, (k % 2 + 1) * packed)
        bus = (iota((near, packed), 0) + (k // 2) * near).astype(F32)
        block = onehot(bus == recv_row[:, side])
        for w in range(2):
            rsum[k * near : (k + 1) * near, w * packed : (w + 1) * packed] = block
        side = slice((k // 2) * packed, (k // 2 + 1) * packed)
        bus = ((iota((packed, 2 * near), 1) & (near - 1)) + (k % 2) * near).astype(F32)
        rback[k * packed : (k + 1) * packed, :] = onehot(bus == recv_col[side])

    link0_row, link1_row = link_ref[0:1, :].astype(F32), link_ref[1:2, :].astype(F32)
    link0, link1 = to_column(link0_row), to_column(link1_row)

    def incidence(index, a, b):
        index = index.astype(F32)
        return jnp.where(index == a, 1.0, 0.0) - jnp.where(index == b, 1.0, 0.0)

    blocks = []
    for k in range(4):
        side = slice((k // 2) * some, (k // 2 + 1) * some)
        bus = (iota((some, 2 * near), 1) & (near - 1)) + (k % 2) * near + dev * buses
        blocks.append(incidence(bus, link0[side], link1[side]))
    ct[...] = jnp.concatenate(blocks, axis=0).astype(BF16)
    zcols = [to_column(imp_ref[ij // 3, ij % 3 : ij % 3 + 1, :]) for ij in range(9)]
    for ij in range(9):
        wide = jnp.broadcast_to(zcols[ij], (buses, cases))
        zpack[ij] = jnp.where(lower(wide[:near]), wide[:near], wide[near:])
    inputs[2].wait()

    def pack_source(step):
        for i in range(3):
            for h, half in enumerate(pack(src[step, i])):
                spack[step, h, i] = half

    pack_source(0)

    def wave_tables():
        first_row, last_row = to_row(first_col), to_row(last_col)
        slot0_col, slot1_col = to_column(slot0_row), to_column(slot1_row)
        seg_sub = iota((segs, lines), 0).astype(F32)
        slot_lane = iota((lines, slots), 1).astype(F32)
        fst = onehot(seg_sub == first_row)
        lst = onehot(seg_sub == last_row)
        gbt[...] = jnp.dot(
            fst, onehot(slot_lane == slot0_col), preferred_element_type=F32
        ).astype(BF16)
        gft[...] = jnp.dot(
            lst, onehot(slot_lane == slot1_col), preferred_element_type=F32
        ).astype(BF16)
        not_first = 1.0 - jnp.sum(fst.astype(F32), axis=1, keepdims=True)
        not_last = 1.0 - jnp.sum(lst.astype(F32), axis=1, keepdims=True)
        for m in range(3):
            r = to_column(refl_ref[m : m + 1, :])
            r_next = pltpu.roll(jnp.broadcast_to(r, (segs, cases)), segs - 1, 0)
            keep_f[m] = jnp.broadcast_to((1.0 - r) * not_first, (segs, cases))
            take_f[m] = jnp.broadcast_to(r * not_first, (segs, cases))
            keep_b[m] = (1.0 - r_next) * not_last
            take_b[m] = r_next * not_last
        single = jnp.where(counts_row == 1.0, 1.0, 0.0)
        a, b = q0.astype(F32) * single, q1.astype(F32) * single
        across = (((1,), (1,)), ((), ()))
        swaps = lax.dot_general(a.astype(BF16), q1, across, preferred_element_type=F32)
        swaps = swaps + lax.dot_general(b.astype(BF16), q0, across, preferred_element_type=F32)
        swaps = swaps.astype(BF16)
        for k in range(4):
            block = swaps[
                (k // 2) * packed : (k // 2 + 1) * packed, (k % 2) * packed : (k % 2 + 1) * packed
            ]
            for w in range(2):
                swap_of[k * packed : (k + 1) * packed, w * packed : (w + 1) * packed] = block

    def advance():
        for m in range(3):
            f, b = fwd[m], bwd[m]
            fwd[m] = keep_f[m] * pltpu.roll(f, 1, 0) + take_f[m] * b
            bwd[m] = keep_b[m] * pltpu.roll(b, segs - 1, 0) + take_b[m] * f

    def scatter(m):
        value = unpack(out[0, m], out[1, m])
        fwd[m] += pick(gbt[...], value)
        bwd[m] += pick(gft[...], value)

    def form_links():
        wait(imp_all, devs - 1, imp_sem.at[1])
        for d in range(devs):
            for i in range(3):
                zrow[3 * i : 3 * i + 3, d * buses : (d + 1) * buses] = imp_all[d, i]
        c = incidence(iota((links, devs * buses), 1), link0, link1)
        c_exact = c.astype(BF16)
        eye = iota((links, links), 0) == iota((links, links), 1)
        for i in range(3):
            for j in range(i + 1):
                z = zrow[3 * i + j : 3 * i + j + 1, :]
                high = z.astype(BF16).astype(F32)
                mid = (z - high).astype(BF16).astype(F32)
                terms = jnp.concatenate([c * high, c * mid, c * (z - high - mid)], axis=0)
                terms = lax.dot_general(
                    terms.astype(BF16), c_exact, (((1,), (1,)), ((), ())), preferred_element_type=F32
                )
                block = terms[:links] + terms[links : 2 * links] + terms[2 * links :]
                if i == j:
                    block = block + jnp.where(eye, resist_ref[...], 0.0)
                for a, b in ((i, j), (j, i))[: 1 + (i != j)]:
                    for k, part in enumerate((near_inv, cross, cross_back, far_inv)):
                        part[a * some : (a + 1) * some, b * some : (b + 1) * some] = block[
                            (k // 2) * some : (k // 2 + 1) * some,
                            (k % 2) * some : (k % 2 + 1) * some,
                        ]

    order = 3 * some
    lane = iota((order, order), 1)

    def eliminate(minv):
        @pl.loop(0, some)
        def _(n):
            spots = [n + w * some for w in range(3)]
            a = minv[...]
            lines_ = [minv[pl.ds(k, 1), :] for k in spots]
            here = [lane == k for k in spots]
            edge = [lane[:1] == k for k in spots]
            cols = [jnp.sum(jnp.where(g, a, 0.0), axis=1, keepdims=True) for g in here]
            block = [
                [jnp.sum(jnp.where(g, r, 0.0), axis=1, keepdims=True) for g in edge]
                for r in lines_
            ]
            for v in range(3):
                inverse = 1.0 / block[v][v]
                row, col = lines_[v], cols[v] * inverse
                a = a - col * row
                scaled = row * inverse
                factor = [block[w][v] for w in range(3)]
                across = [block[v][w] * inverse for w in range(3)]
                for w in range(3):
                    lines_[w] = scaled if w == v else lines_[w] - factor[w] * scaled
                    cols[w] = col if w == v else cols[w] - block[v][w] * col
                for w in range(3):
                    for x in range(3):
                        if w != v and x != v:
                            block[w][x] = block[w][x] - factor[w] * across[x]
                for w in range(3):
                    if w != v:
                        block[w][v], block[v][w] = factor[w] * inverse, across[w]
                block[v][v] = -inverse
            for w in range(3):
                a = jnp.where(here[w], cols[w], a)
                for x in range(3):
                    lines_[w] = jnp.where(edge[x], block[w][x], lines_[w])
            minv[...] = a
            for w in range(3):
                minv[pl.ds(spots[w], 1), :] = lines_[w]

    def exact_dot(a, b):
        return jnp.dot(a, b, precision=EXACT, preferred_element_type=F32)

    def reduce_far():
        ahead[...] = exact_dot(near_inv[...], cross[...])
        far_inv[...] += exact_dot(cross_back[...], ahead[...])

    def link_effect():
        back = exact_dot(cross_back[...], near_inv[...])
        corner = exact_dot(ahead[...], far_inv[...])
        parts = (
            (0, 0, near_inv[...] + exact_dot(corner, back)),
            (0, 1, corner),
            (1, 0, exact_dot(far_inv[...], back)),
            (1, 1, far_inv[...]),
        )
        inverse[...] = jnp.zeros_like(inverse)
        for a, b, part in parts:
            for k in range(3):
                inverse[
                    k, a * some : (a + 1) * some, b * cases : b * cases + 3 * some
                ] = part[k * some : (k + 1) * some]
        c = incidence(iota((buses, links), 0) + dev * buses, link0_row, link1_row)
        drops = [exact_dot(c, inverse[k]) for k in range(3)]
        for i in range(3):
            effect = zcols[3 * i] * drops[0] + zcols[3 * i + 1] * drops[1]
            effect = effect + zcols[3 * i + 2] * drops[2]
            for w, part in enumerate(high_low(effect)):
                for k in range(4):
                    spot = (4 * w + k) * 3 * near + i * near
                    u[spot : spot + near, :] = part[
                        (k // 2) * near : (k // 2 + 1) * near,
                        (k % 2) * cases : (k % 2) * cases + 3 * some,
                    ]

    def apply(values):
        return [
            zpack[3 * i] * values[0] + zpack[3 * i + 1] * values[1] + zpack[3 * i + 2] * values[2]
            for i in range(3)
        ]

    def share(step, h):
        wait(h_recv.at[step, h], total - 1, recv_sem.at[0, step, h])
        parts = [h_recv[step, h, :, i].reshape(packed, cases) for i in range(3)]
        total_in = packed_dot(rsum[...], parts)
        volts = apply([spack[step, h, i] + total_in[i] for i in range(3)])
        for i in range(3):
            open_volts[h, i] = volts[i]
        opened = packed_dot(ct[...], volts)
        for i in range(3):
            e_recv[step, h, dev // 2, i * some : (i + 1) * some, :] = opened[i]

        @pl.loop(1, devs // 2, unroll=devs <= 8)
        def _(p):
            pltpu.make_async_remote_copy(
                src_ref=e_recv.at[step, h, dev // 2],
                dst_ref=e_recv.at[step, h, dev // 2],
                send_sem=send_sem.at[1, step, h],
                recv_sem=recv_sem.at[1, step, h],
                device_id=(area, dev ^ (devs - 2 * p)),
                device_id_type=MESH,
            ).start()

    def settle(step, h, meanwhile=None):
        wait(e_recv.at[step, h], devs // 2 - 1, recv_sem.at[1, step, h])
        own = lax.rem(dev, 2)
        e_pair[step, h, own] = jnp.sum(e_recv[step, h], axis=0)
        swap_sum = pltpu.make_async_remote_copy(
            src_ref=e_pair.at[step, h, own],
            dst_ref=e_pair.at[step, h, own],
            send_sem=send_sem.at[3, step, h],
            recv_sem=recv_sem.at[3, step, h],
            device_id=(area, dev ^ 1),
            device_id_type=MESH,
        )
        swap_sum.start()
        if meanwhile is not None:
            meanwhile()
        swap_sum.wait()
        opened = e_pair[step, h, 0] + e_pair[step, h, 1]
        result = jnp.dot(
            u[...], jnp.concatenate(high_low(opened), axis=1), preferred_element_type=F32
        )
        main = 12 * near
        change = fold(result[:main, :cases] + result[:main, cases:] + result[main:, :cases])
        volts = [open_volts[h, i] + change[i * near : (i + 1) * near] for i in range(3)]
        half = cases // 2
        mine = slice(h * half, (h + 1) * half)
        for i in range(3):
            turned = swap(volts[i])
            low, high = (volts[i], turned) if h == 0 else (turned, volts[i])
            volt[step, i, :near, mine] = low[:, mine]
            volt[step, i, near:, mine] = high[:, mine]
        sent = packed_dot(rback[...], volts)
        for i in range(3):
            v_send[step, h, :, i] = sent[i].reshape(total, few, cases)
        push_all(v_send, v_recv, 2, step, h)

    def leave(step, h):
        wait(v_recv.at[step, h], total - 1, recv_sem.at[2, step, h])
        ends = [v_recv[step, h, :, i].reshape(packed, cases) for i in range(3)]
        results = []
        for m in range(3):
            value = trans_ref[m, 0] * ends[0] + trans_ref[m, 1] * ends[1] + trans_ref[m, 2] * ends[2]
            value = value - arr[h, m]
            out[h, m] = value
            results.append(value)
        return results

    def volt_copy(step):
        return pltpu.make_async_copy(volt.at[step], volt_out.at[step], out_sem.at[step])

    form_links()
    eliminate(near_inv)
    share(0, 0)
    reduce_far()
    share(0, 1)
    eliminate(far_inv)
    link_effect()
    for h in range(HALVES):
        settle(0, h)
    volt_copy(0).start()
    wave_tables()
    advance()
    gather(nxt)

    @pl.loop(1, STEPS)
    def _(step):
        for h in range(HALVES):
            moved = packed_dot(swap_of[...], leave(step - 1, h))
            for m in range(3):
                arr[h, m] = nxt[h, m] + moved[m]
            inject(step, h)
            push_all(h_send, h_recv, 0, step, h)
        pack_source(step)
        share(step, 0)
        for m in range(3):
            scatter(m)
        advance()
        share(step, 1)
        settle(step, 0, lambda: pl.when(step < STEPS - 1)(lambda: gather(nxt)))
        settle(step, 1)
        volt_copy(step).start()

    for h in range(HALVES):
        leave(STEPS - 1, h)
    outputs = []
    for m in range(3):
        scatter(m)
        for k, (a, b) in enumerate(((fwd, fwd_out), (bwd, bwd_out))):
            outputs.append(
                pltpu.make_async_copy(a.at[m], b.at[m], out_sem.at[STEPS + 2 * m + k])
            )
            outputs[-1].start()

    wait(imp_all, devs - 1, imp_sem.at[0])

    @pl.loop(0, STEPS)
    def _(step):
        volt_copy(step).wait()
        for h in range(HALVES):
            wait(h_send.at[step, h], total - 1, send_sem.at[0, step, h])
            wait(e_recv.at[step, h], devs // 2 - 1, send_sem.at[1, step, h])
            wait(v_send.at[step, h], total - 1, send_sem.at[2, step, h])

    for copy in outputs:
        copy.wait()


def hand_over(volt_in, fwd_in, bwd_in, volt_out, fwd_out, bwd_out, volt, fwd, bwd, sems):
    groups = ((fwd_in, fwd, fwd_out), (bwd_in, bwd, bwd_out), (volt_in, volt, volt_out))
    copies = [
        (
            pltpu.make_async_copy(a.at[n], b.at[n], sems.at[0, k, n]),
            pltpu.make_async_copy(b.at[n], c.at[n], sems.at[1, k, n]),
        )
        for k, (a, b, c) in enumerate(groups)
        for n in range(a.shape[0])
    ]
    for first, _ in copies:
        first.start()
    for first, second in copies:
        first.wait()
        second.start()
    for _, second in copies:
        second.wait()


def on_device(
    areas,
    devs,
    wave_fwd,
    wave_bwd,
    seg_reflect,
    seg_count,
    modal_admit,
    modal_transform,
    end_slot,
    recv_bus,
    bus_impedance,
    link_bus,
    link_resist,
    source_current,
):
    total = areas * devs
    cases, segs = wave_fwd.shape[2], wave_fwd.shape[1]
    cap = recv_bus.shape[1] // total
    rows = -(-cap // 8) * 8
    if rows != cap:
        end_slot = end_slot // cap * rows + end_slot % cap
        recv_bus = jnp.pad(
            recv_bus.reshape(total, cap), ((0, 0), (0, rows - cap)), constant_values=-1
        ).reshape(1, total * rows)
    slots = total * rows
    buses = bus_impedance.shape[2]
    links = link_bus.shape[0]
    vmem = pl.BlockSpec(memory_space=pltpu.VMEM)
    smem = pl.BlockSpec(memory_space=pltpu.SMEM)
    anywhere = pl.BlockSpec(memory_space=pl.ANY)
    volt_shape = (STEPS, 3, buses, cases)
    sent = (STEPS, HALVES, total, 3, rows // 2, cases)
    half_slots = (HALVES, 3, slots // 2, cases)
    results = pl.pallas_call(
        functools.partial(kernel, areas, devs),
        out_shape=(
            jax.ShapeDtypeStruct(volt_shape, F32),
            jax.ShapeDtypeStruct(wave_fwd.shape, F32),
            jax.ShapeDtypeStruct(wave_bwd.shape, F32),
        ),
        in_specs=[anywhere] * 2 + [vmem] * 3 + [smem] + [vmem] * 5 + [anywhere],
        out_specs=(anywhere, anywhere, anywhere),
        scratch_shapes=[
            pltpu.VMEM(wave_fwd.shape, F32),
            pltpu.VMEM(wave_bwd.shape, F32),
            pltpu.VMEM(volt_shape, F32),
            pltpu.VMEM(volt_shape, F32),
            pltpu.VMEM(sent, F32),
            pltpu.VMEM(sent, F32),
            pltpu.VMEM((STEPS, HALVES, devs // 2, 3 * links // 2, cases), F32),
            pltpu.VMEM((STEPS, HALVES, 2, 3 * links // 2, cases), F32),
            pltpu.VMEM(sent, F32),
            pltpu.VMEM(sent, F32),
            pltpu.VMEM((devs, 3, 3, buses), F32),
            pltpu.VMEM((16, devs * buses), F32),
            pltpu.VMEM((slots, 2 * segs), BF16),
            pltpu.VMEM((2 * slots, slots), BF16),
            pltpu.VMEM((segs, slots), BF16),
            pltpu.VMEM((segs, slots), BF16),
            pltpu.VMEM((2 * buses, slots), BF16),
            pltpu.VMEM((2 * slots, buses), BF16),
            pltpu.VMEM((2 * links, buses), BF16),
            pltpu.VMEM((12 * buses, 3 * links // 2), BF16),
            pltpu.VMEM((3, slots // 2, cases), F32),
            pltpu.VMEM((9, buses // 2, cases), F32),
            pltpu.VMEM((STEPS, HALVES, 3, buses // 2, cases), F32),
            pltpu.VMEM((3, segs, cases), F32),
            pltpu.VMEM((3, segs, cases), F32),
            pltpu.VMEM((3, segs, cases), F32),
            pltpu.VMEM((3, segs, cases), F32),
            pltpu.VMEM(half_slots, F32),
            pltpu.VMEM(half_slots, F32),
            pltpu.VMEM(half_slots, F32),
            pltpu.VMEM((HALVES, 3, buses // 2, cases), F32),
            *[pltpu.VMEM((3 * links // 2, 3 * links // 2), F32)] * 5,
            pltpu.VMEM((3, links, 2 * cases), F32),
            pltpu.SemaphoreType.DMA((4, STEPS, HALVES)),
            pltpu.SemaphoreType.DMA((4, STEPS, HALVES)),
            pltpu.SemaphoreType.DMA((2,)),
            pltpu.SemaphoreType.DMA((3,)),
            pltpu.SemaphoreType.DMA((STEPS + 6,)),
        ],
        compiler_params=pltpu.CompilerParams(
            collective_id=0, has_side_effects=True, vmem_limit_bytes=60 * 1024 * 1024
        ),
        name="transient",
    )(
        wave_fwd,
        wave_bwd,
        seg_reflect,
        seg_count,
        modal_admit,
        modal_transform,
        end_slot.T,
        recv_bus,
        bus_impedance,
        link_bus.T,
        link_resist.reshape(1, links),
        jnp.transpose(source_current, (0, 2, 1, 3)),
    )
    volts, fwd, bwd = pl.pallas_call(
        hand_over,
        out_shape=tuple(jax.ShapeDtypeStruct(a.shape, F32) for a in results),
        in_specs=[anywhere] * 3,
        out_specs=(anywhere,) * 3,
        scratch_shapes=[pltpu.VMEM(a.shape, F32) for a in results]
        + [pltpu.SemaphoreType.DMA((2, 3, STEPS))],
        name="hand_over",
    )(*results)
    return (jnp.transpose(volts, (0, 2, 1, 3)), fwd, bwd)


def solution(mesh):
    in_specs = (
        P(None, ("area", "dev"), None),
        P(None, ("area", "dev"), None),
        P(None, ("area", "dev")),
        P(("area", "dev"), None),
        P(None, ("area", "dev")),
        P(),
        P(("area", "dev"), None),
        P(("area", "dev"), None),
        P(None, None, ("area", "dev")),
        P("area", None),
        P("area"),
        P(None, ("area", "dev"), None, None),
    )
    out_specs = (
        P(None, ("area", "dev"), None, None),
        P(None, ("area", "dev"), None),
        P(None, ("area", "dev"), None),
    )
    return jax.shard_map(
        functools.partial(on_device, mesh.shape["area"], mesh.shape["dev"]),
        mesh=mesh,
        in_specs=in_specs,
        out_specs=out_specs,
        check_vma=False,
    )
```
